256 devices in a mesh: ctx: 16 (over z, y_hi), fsdp: 16 (over x, y_lo, core).
Axes of the slice: x: 4, y: 4 (y_hi: 2, y_lo: 2; y = y_hi * 2 + y_lo), z: 8, core: 2. Of those that a mesh axis runs over, the one named last changes fastest.
Arguments:
- queries: bfloat16 [16, 2, 2048, 2048], P('fsdp', None, 'ctx'), may hold values from -20 to 20
- keys: bfloat16 [16, 2, 2048, 2048], P('fsdp', None, 'ctx'), may hold values from -20 to 20
- values: bfloat16 [16, 2, 2048, 2048], P('fsdp', None, 'ctx'), may hold values from -6 to 6
- docs: int32 [16, 2048], P('fsdp'), may hold values from 0 to 3, never falling along the last dimension, each value on 1 to 1024 neighbouring positions
- layout: int32 [16], replicated, may hold values from 0 to 15, each once
- w_out: bfloat16 [2048, 4096], P('fsdp'), may hold values from -0.75 to 0.75
Outputs:
- mixed: bfloat16 [16, 2, 2048, 4096], P('fsdp', None, 'ctx')
The draws below stay inside these ranges and needn't reach their ends.
All inputs are finite; a program needn't handle non-finite values.
Results may differ from the reference program's by a relative error of at most 0.007.
Values may be sent and summed in bfloat16 or wider, within the bound.
A program may use at most 192 MiB of HBM per device.

```python
import math
import jax
import jax.numpy as jnp
import numpy as np
from jax import lax

MODEL_DIM = 4096
HEAD_DIM = 128
HEADS = 16
BLOCK = 16
GROUP = 128
INNER = 2048
LENGTH = 2048
SEQS = 16
N_CTX = 16


def draw_queries(key, part):
    key = jax.random.fold_in(key, 11)
    result = jnp.clip(jax.random.normal(key, (SEQS, 2, LENGTH, INNER), jnp.float32), -6.0, 6.0)
    return result.astype(jnp.bfloat16)


def draw_keys(key, part):
    key = jax.random.fold_in(key, 23)
    result = jnp.clip(jax.random.normal(key, (SEQS, 2, LENGTH, INNER), jnp.float32), -6.0, 6.0)
    return result.astype(jnp.bfloat16)


def block_scale(key, shape, pieces, smallest, high):
    def one(dim, parts):
        steps = jax.random.uniform(jax.random.fold_in(jax.random.fold_in(key, 6), dim), (parts,), jnp.float32, smallest / len(pieces), high / len(pieces))
        return jnp.repeat(jnp.exp(steps), shape[dim] // parts).reshape((-1,) + (1,) * (len(shape) - dim - 1))

    level = one(*pieces[0])
    for cut in pieces[1:]:
        level = level * one(*cut)
    return level


def profile(amount, total, most, slope):
    loads = [(1 << 20) // math.isqrt(grade ** slope) + 1 for grade in range(2, amount + 1)]
    rest, counts = total - most - (amount - 1), [1] * (amount - 1)
    while rest > 0:
        movable = [i for i in range(amount - 1) if counts[i] < most]
        mass, remaining = sum([loads[i] for i in movable]), rest
        for i in movable:
            more = min(most - counts[i], max(1, remaining * loads[i] // mass), rest)
            counts[i] = counts[i] + more
            rest = rest - more
    return np.array([most] + counts)


def uneven(rng, count, total, reach, slope):
    if count == 2:
        one = jax.random.randint(rng, (), max(1, total - reach), min(reach, total - 1) + 1)
        return jnp.stack([one, total - one])
    tallies = jnp.asarray(profile(count, total, reach, slope), jnp.int32)
    couples = (count - 1) // 2
    donor, taker = tallies[1:1 + 2 * couples:2], tallies[2:2 + 2 * couples:2]
    slack = jnp.minimum(donor - 1, reach - taker)
    moved = jax.random.randint(jax.random.fold_in(rng, 1), (couples,), 0, 1 << 20) % (slack + 1)
    tallies = tallies.at[1:1 + 2 * couples:2].set(donor - moved).at[2:2 + 2 * couples:2].set(taker + moved)
    return tallies[jax.random.permutation(jax.random.fold_in(rng, 2), count)]


def normal_values(key, dims, width, reach, split=(), held_as=jnp.bfloat16):
    values = jax.random.normal(key, dims, jnp.float32) * width
    if len(split) > 0:
        values = block_scale(key, dims, split, -0.22, 0.18) * values
    return jnp.clip(values, min=-reach, max=reach).astype(held_as)


def setup_inputs(seed: int = 0) -> dict:
    seeds = jax.random.split(jax.random.key(seed), 7)
    return {
        "queries": draw_queries(jax.random.fold_in(seeds[6], 71), 0),
        "keys": draw_keys(jax.random.fold_in(seeds[6], 71), 0),
        "values": normal_values(seeds[2], (SEQS, 2, LENGTH, INNER), 1.0, 6.0, ((0, 16), (2, 16))),
        "docs": jax.vmap(lambda own: jnp.searchsorted(jnp.cumsum(uneven(own, 4, LENGTH, LENGTH // 2, 0)), jnp.arange(LENGTH), side="right"))(jax.random.split(seeds[3], SEQS)).reshape((SEQS, LENGTH)).astype(jnp.int32),
        "layout": jax.random.permutation(seeds[4], N_CTX).astype(jnp.int32),
        "w_out": normal_values(seeds[5], (INNER, MODEL_DIM), 64 ** -0.5, 0.75, ((0, 16),)),
    }


def reference(queries, keys, values, docs, layout, w_out):
    index = jnp.arange(LENGTH, dtype=jnp.int32)
    position = (layout[index // GROUP] * GROUP + index % GROUP).astype(jnp.int32)
    block_of = position // BLOCK
    both_blocks = jnp.concatenate([block_of, block_of])
    is_clean = jnp.arange(2 * LENGTH, dtype=jnp.int32) < LENGTH
    scaling = 1.0 / math.sqrt(HEAD_DIM)

    def one_sequence(operands):
        query_row, key_row, value_row, doc_row = operands
        doc_at = doc_row[position]
        doc_both = jnp.concatenate([doc_at, doc_at])
        same_doc = doc_both[:, None] == doc_both[None, :]
        query_clean = is_clean[:, None]
        key_clean = is_clean[None, :]
        query_block = both_blocks[:, None]
        key_block = both_blocks[None, :]
        allowed = same_doc & (query_clean & key_clean & (key_block <= query_block) | ~query_clean & key_clean & (key_block < query_block) | ~query_clean & ~key_clean & (key_block == query_block))
        query_flat = query_row.reshape(2 * LENGTH, INNER)
        key_flat = key_row.reshape(2 * LENGTH, INNER)
        value_flat = value_row.reshape(2 * LENGTH, INNER)

        def one_head(head_index):
            start = (head_index * HEAD_DIM).astype(jnp.int32)
            query_head = lax.dynamic_slice_in_dim(query_flat, start, HEAD_DIM, 1)
            key_head = lax.dynamic_slice_in_dim(key_flat, start, HEAD_DIM, 1)
            value_head = lax.dynamic_slice_in_dim(value_flat, start, HEAD_DIM, 1)
            scores = jnp.dot(query_head, key_head.T, preferred_element_type=jnp.float32) * scaling
            masked = jnp.where(allowed, scores, -jnp.inf)
            largest = lax.optimization_barrier(jnp.max(masked, axis=1))
            weights = jnp.where(allowed, jnp.exp(scores - largest[:, None]), 0.0)
            totals = lax.optimization_barrier(jnp.sum(weights, axis=1))
            summed = jnp.dot(weights.astype(jnp.bfloat16), value_head, preferred_element_type=jnp.float32)
            return (summed / totals[:, None]).astype(jnp.bfloat16)
        context = lax.map(one_head, jnp.arange(HEADS, dtype=jnp.int32))
        context = jnp.transpose(context, (1, 0, 2)).reshape(2 * LENGTH, INNER)
        mixed = jnp.dot(context, w_out, preferred_element_type=jnp.float32).astype(jnp.bfloat16)
        return mixed.reshape(2, LENGTH, MODEL_DIM)
    return lax.map(one_sequence, (queries, keys, values, docs))
```

```python
import functools
import math

import jax
import jax.numpy as jnp
from jax import lax
from jax.experimental import pallas as pl
from jax.experimental.pallas import tpu as pltpu
from jax.sharding import PartitionSpec as P

MESH = pl.DeviceIdType.MESH
HEAD = 128
GROUP = 128
BLOCK = 16
N = 16
WINDOW = 1024 // GROUP + 1
MASKED = -1e30
FLOOR = -1e20
TINY = 1e-30
C2 = math.log2(math.e) / math.sqrt(HEAD)


def offset(step):
    zi, dy = step // 2, step % 2
    dz = ((zi + 1) // 2) * (2 * (zi % 2) - 1)
    return dz, dy


def peer(step, sign):
    me = lax.axis_index("ctx")
    dz, dy = offset(step)
    z = (me // 2 + sign * dz + N) % (N // 2)
    return z * 2 + (me % 2 + dy) % 2


def column_of(row):
    return jnp.transpose(jnp.broadcast_to(row, (GROUP, row.shape[1])), (1, 0))


def kernel(
    layout, docs, q, k, v, out,
    q_all, k_all, v_all, vt_all, o_snd, lse_snd, o_rcv, lse_rcv,
    qn, kn, vn, o2, lse2, doc_rows, doc_cols, scores, inv,
    q_ss, k_ss, v_ss, o_ss, l_ss, q_rs, k_rs, v_rs, o_rs, l_rs, loc,
):
    me = lax.axis_index("ctx")
    fs = lax.axis_index("fsdp")

    def lanes(h):
        return pl.ds(pl.multiple_of(h * HEAD, HEAD), HEAD)

    barrier = pltpu.get_barrier_semaphore()
    for t in range(1, N):
        pl.semaphore_signal(barrier, inc=1, device_id=(peer(t, 1), fs), device_id_type=MESH)

    local = [
        pltpu.make_async_copy(k.at[0, 0, :, lanes(me)], k_all.at[me], loc.at[0]),
        pltpu.make_async_copy(v.at[0, 0, :, lanes(me)], v_all.at[me], loc.at[1]),
        pltpu.make_async_copy(q.at[0, :, :, lanes(me)], q_all.at[me], loc.at[2]),
        pltpu.make_async_copy(q.at[0, 1], qn, loc.at[3]),
        pltpu.make_async_copy(k.at[0, 1], kn, loc.at[4]),
        pltpu.make_async_copy(v.at[0, 1], vn, loc.at[5]),
    ]
    pl.semaphore_wait(barrier, N - 1)

    def send_k(j, s):
        return pltpu.make_async_remote_copy(
            src_ref=k.at[0, 0, :, lanes(j)], dst_ref=k_all.at[s], send_sem=k_ss.at[j],
            recv_sem=k_rs.at[s], device_id=(j, fs), device_id_type=MESH)

    def send_v(j, s):
        return pltpu.make_async_remote_copy(
            src_ref=v.at[0, 0, :, lanes(j)], dst_ref=v_all.at[s], send_sem=v_ss.at[j],
            recv_sem=v_rs.at[s], device_id=(j, fs), device_id_type=MESH)

    def send_q(j, s):
        return pltpu.make_async_remote_copy(
            src_ref=q.at[0, :, :, lanes(j)], dst_ref=q_all.at[s], send_sem=q_ss.at[j],
            recv_sem=q_rs.at[s], device_id=(j, fs), device_id_type=MESH)

    def send_o(j, s):
        return pltpu.make_async_remote_copy(
            src_ref=o_snd.at[j], dst_ref=o_rcv.at[s], send_sem=o_ss.at[j],
            recv_sem=o_rs.at[s], device_id=(j, fs), device_id_type=MESH)

    def send_l(j, s):
        return pltpu.make_async_remote_copy(
            src_ref=lse_snd.at[j], dst_ref=lse_rcv.at[s], send_sem=l_ss.at[j],
            recv_sem=l_rs.at[s], device_id=(j, fs), device_id_type=MESH)

    @pl.loop(1, N)
    def _(t):
        j = peer(t, 1)
        send_k(j, me).start()
        send_v(j, me).start()

    @pl.loop(1, N)
    def _(t):
        send_q(peer(t, 1), me).start()

    for copy in local:
        copy.start()

    for g in range(N):
        row = docs[:, g * GROUP:(g + 1) * GROUP]
        doc_rows[g] = row.astype(jnp.float32)

    @pl.loop(0, N)
    def _(g):
        found = jnp.int32(0)
        for c in range(N):
            found = jnp.where(layout[c] == g, c, found)
        inv[g] = found

    @pl.loop(0, N)
    def _(g):
        doc_cols[g] = column_of(doc_rows[g])

    key_block = lax.broadcasted_iota(jnp.int32, (GROUP, GROUP), 0) // BLOCK
    query_block = lax.broadcasted_iota(jnp.int32, (GROUP, GROUP), 1) // BLOCK

    for copy in local[3:]:
        copy.wait()
    mine = layout[me]
    home = (doc_cols[mine] == doc_rows[mine]) & (key_block == query_block)

    @pl.loop(0, N)
    def _(h):
        s = lax.dot_general(kn[:, lanes(h)], qn[:, lanes(h)], (((1,), (1,)), ((), ())),
                            preferred_element_type=jnp.float32)
        s = jnp.where(home, s, MASKED)
        top = jnp.max(s, axis=0, keepdims=True)
        p = jnp.exp2((s - top) * C2)
        total = jnp.sum(p, axis=0, keepdims=True)
        o = lax.dot_general(vn[:, lanes(h)], p.astype(jnp.bfloat16), (((0,), (0,)), ((), ())),
                            preferred_element_type=jnp.float32)
        o2[h] = o / total
        lse2[h] = top * C2 + jnp.log2(total)

    for copy in local[:2]:
        copy.wait()

    @pl.loop(1, N)
    def _(t):
        s = peer(t, -1)
        send_k(s, s).wait_recv()
        send_v(s, s).wait_recv()

    @pl.loop(0, N)
    def _(g):
        vt_all[g] = jnp.transpose(v_all[g].astype(jnp.float32), (1, 0)).astype(jnp.bfloat16)

    local[2].wait()

    @pl.loop(0, N)
    def _(t):
        d = peer(t, -1)

        @pl.when(t > 0)
        def _():
            send_q(d, d).wait_recv()

        p_q = layout[d]
        queries = q_all[d].reshape(2 * GROUP, HEAD)
        doc_q = doc_rows[p_q]
        places = []
        top = jnp.full((1, 2 * GROUP), FLOOR, jnp.float32)
        for w in range(WINDOW):
            at = (p_q - w + N) % N
            place = inv[at]
            places.append(place)
            s = lax.dot_general(k_all[place], queries, (((1,), (1,)), ((), ())),
                                preferred_element_type=jnp.float32)
            wanted = jnp.where(p_q >= w, doc_q, -1.0)
            same = doc_cols[at] == wanted
            if w == 0:
                clean = same & (key_block <= query_block)
                noisy = same & (key_block < query_block)
            else:
                clean = noisy = same
            s = jnp.concatenate([jnp.where(clean, s[:, :GROUP], MASKED), jnp.where(noisy, s[:, GROUP:], MASKED)], axis=1)
            scores[w] = s
            top = jnp.maximum(top, jnp.max(s, axis=0, keepdims=True))
        total = jnp.zeros((1, 2 * GROUP), jnp.float32)
        o = jnp.zeros((HEAD, 2 * GROUP), jnp.float32)
        for w in range(WINDOW):
            p = jnp.exp2((scores[w] - top) * C2)
            total = total + jnp.sum(p, axis=0, keepdims=True)
            o = o + jnp.dot(vt_all[places[w]], p.astype(jnp.bfloat16), preferred_element_type=jnp.float32)
        safe = jnp.maximum(total, TINY)
        o_snd[d] = (o / safe).astype(jnp.bfloat16)
        lse_snd[d] = jnp.broadcast_to(top * C2 + jnp.log2(safe), (8, 2 * GROUP))

        @pl.when(t > 0)
        def _():
            send_o(d, me).start()
            send_l(d, me).start()

        @pl.when(t == 0)
        def _():
            o_rcv[me] = o_snd[d]
            lse_rcv[me] = lse_snd[d]

    @pl.loop(0, N)
    def _(t):
        h = peer(t, -1)

        @pl.when(t > 0)
        def _():
            send_o(h, h).wait_recv()
            send_l(h, h).wait_recv()

        lse1 = lse_rcv[h][0:1, GROUP:]
        lse_n = lse2[h]
        high = jnp.maximum(lse1, lse_n)
        e1 = jnp.exp2(lse1 - high)
        e2 = jnp.exp2(lse_n - high)
        both = e1 + e2
        clean = o_rcv[h][:, :GROUP].astype(jnp.float32)
        noisy = o_rcv[h][:, GROUP:].astype(jnp.float32) * (e1 / both) + o2[h] * (e2 / both)
        out[:GROUP, lanes(h)] = jnp.transpose(clean, (1, 0)).astype(jnp.bfloat16)
        out[GROUP:, lanes(h)] = jnp.transpose(noisy, (1, 0)).astype(jnp.bfloat16)

    @pl.loop(1, N)
    def _(t):
        j = peer(t, 1)
        send_k(j, me).wait_send()
        send_v(j, me).wait_send()
        send_q(j, me).wait_send()
        send_o(j, me).wait_send()
        send_l(j, me).wait_send()


def local(queries, keys, values, docs, layout, w_out):
    vm = lambda *shape: pltpu.VMEM(shape, jnp.bfloat16)
    vf = lambda *shape: pltpu.VMEM(shape, jnp.float32)
    sems = [pltpu.SemaphoreType.DMA((N,))] * 10
    any_spec = pl.BlockSpec(memory_space=pltpu.HBM)
    context = pl.pallas_call(
        kernel,
        out_shape=jax.ShapeDtypeStruct((2 * GROUP, N * HEAD), jnp.bfloat16),
        in_specs=[
            pl.BlockSpec(memory_space=pltpu.SMEM),
            pl.BlockSpec(memory_space=pltpu.VMEM),
            any_spec, any_spec, any_spec,
        ],
        out_specs=pl.BlockSpec(memory_space=pltpu.VMEM),
        scratch_shapes=[
            vm(N, 2, GROUP, HEAD), vm(N, GROUP, HEAD), vm(N, GROUP, HEAD), vm(N, HEAD, GROUP),
            vm(N, HEAD, 2 * GROUP), vf(N, 8, 2 * GROUP), vm(N, HEAD, 2 * GROUP), vf(N, 8, 2 * GROUP),
            vm(GROUP, N * HEAD), vm(GROUP, N * HEAD), vm(GROUP, N * HEAD),
            vf(N, HEAD, GROUP), vf(N, 1, GROUP), vf(N, 1, GROUP), vf(N, GROUP, GROUP),
            vf(WINDOW, GROUP, 2 * GROUP), pltpu.SMEM((N,), jnp.int32),
            *sems, pltpu.SemaphoreType.DMA((6,)),
        ],
        compiler_params=pltpu.CompilerParams(
            collective_id=0, has_side_effects=True, vmem_limit_bytes=48 * 2 ** 20),
        cost_estimate=pl.CostEstimate(flops=3 * 10 ** 9, bytes_accessed=8 * 10 ** 6, transcendentals=5 * 10 ** 6),
    )(layout, docs, queries, keys, values)
    mixed = jnp.dot(
        context,
        lax.all_gather(w_out, "fsdp", axis=0, tiled=True),
        preferred_element_type=jnp.float32,
    )
    return mixed.astype(jnp.bfloat16).reshape(1, 2, GROUP, w_out.shape[1])


def solution(mesh):
    return jax.shard_map(
        local,
        mesh=mesh,
        in_specs=(
            P("fsdp", None, "ctx", None),
            P("fsdp", None, "ctx", None),
            P("fsdp", None, "ctx", None),
            P("fsdp", None),
            P(),
            P("fsdp", None),
        ),
        out_specs=P("fsdp", None, "ctx", None),
        check_vma=False,
    )
```

```python
import functools
import math

import jax
import jax.numpy as jnp
from jax import lax
from jax.experimental import pallas as pl
from jax.experimental.pallas import tpu as pltpu
from jax.sharding import PartitionSpec as P

MESH = pl.DeviceIdType.MESH
HEAD = 128
GROUP = 128
BLOCK = 16
N = 16
WINDOW = 1024 // GROUP + 1
MASKED = -1e30
FLOOR = -1e20
TINY = 1e-30
TILE = 512
C2 = math.log2(math.e) / math.sqrt(HEAD)


def offset(step):
    zi, dy = step // 2, step % 2
    dz = ((zi + 1) // 2) * (2 * (zi % 2) - 1)
    return dz, dy


def peer(step, sign):
    me = lax.axis_index("ctx")
    dz, dy = offset(step)
    z = (me // 2 + sign * dz + N) % (N // 2)
    return z * 2 + (me % 2 + dy) % 2


def column_of(row):
    return jnp.transpose(jnp.broadcast_to(row, (GROUP, row.shape[1])), (1, 0))


def kernel(
    layout, docs, q, k, v, w, out,
    w_all, ctx, q_all, k_all, v_all, vt_all, o_snd, lse_snd, o_rcv, lse_rcv,
    qn, kn, vn, o2, lse2, doc_rows, doc_cols, scores, inv,
    q_ss, k_ss, v_ss, o_ss, l_ss, q_rs, k_rs, v_rs, o_rs, l_rs, loc, w_ss, w_rs,
):
    me = lax.axis_index("ctx")
    fs = lax.axis_index("fsdp")

    def lanes(h):
        return pl.ds(pl.multiple_of(h * HEAD, HEAD), HEAD)

    kin = (fs // 2) * 2 + (fs + 1) % 2
    across = (fs // 4) * 4 + (fs + 2) % 4
    right, left, far = (fs + 4) % N, (fs + 12) % N, (fs + 8) % N
    twin = (me // 2) * 2 + (me + 1) % 2
    beside = {"kin": (me, kin), "right": (me, right), "left": (me, left), "near": (me, across), "away": (twin, across)}

    barrier = pltpu.get_barrier_semaphore()
    for name in beside:
        pl.semaphore_signal(barrier, inc=1, device_id=beside[name], device_id_type=MESH)
    for t in range(1, N):
        pl.semaphore_signal(barrier, inc=1, device_id=(peer(t, 1), fs), device_id_type=MESH)

    local = [
        pltpu.make_async_copy(k.at[0, 0, :, lanes(me)], k_all.at[me], loc.at[0]),
        pltpu.make_async_copy(v.at[0, 0, :, lanes(me)], v_all.at[me], loc.at[1]),
        pltpu.make_async_copy(q.at[0, :, :, lanes(me)], q_all.at[me], loc.at[2]),
        pltpu.make_async_copy(q.at[0, 1], qn, loc.at[3]),
        pltpu.make_async_copy(k.at[0, 1], kn, loc.at[4]),
        pltpu.make_async_copy(v.at[0, 1], vn, loc.at[5]),
        pltpu.make_async_copy(w, w_all.at[fs], loc.at[6]),
    ]
    pl.semaphore_wait(barrier, N - 1 + len(beside))

    def send_k(j, s):
        return pltpu.make_async_remote_copy(
            src_ref=k.at[0, 0, :, lanes(j)], dst_ref=k_all.at[s], send_sem=k_ss.at[j],
            recv_sem=k_rs.at[s], device_id=(j, fs), device_id_type=MESH)

    def send_v(j, s):
        return pltpu.make_async_remote_copy(
            src_ref=v.at[0, 0, :, lanes(j)], dst_ref=v_all.at[s], send_sem=v_ss.at[j],
            recv_sem=v_rs.at[s], device_id=(j, fs), device_id_type=MESH)

    def send_q(j, s):
        return pltpu.make_async_remote_copy(
            src_ref=q.at[0, :, :, lanes(j)], dst_ref=q_all.at[s], send_sem=q_ss.at[j],
            recv_sem=q_rs.at[s], device_id=(j, fs), device_id_type=MESH)

    def send_o(j, s):
        return pltpu.make_async_remote_copy(
            src_ref=o_snd.at[j], dst_ref=o_rcv.at[s], send_sem=o_ss.at[j],
            recv_sem=o_rs.at[s], device_id=(j, fs), device_id_type=MESH)

    def send_l(j, s):
        return pltpu.make_async_remote_copy(
            src_ref=lse_snd.at[j], dst_ref=lse_rcv.at[s], send_sem=l_ss.at[j],
            recv_sem=l_rs.at[s], device_id=(j, fs), device_id_type=MESH)

    @pl.loop(1, N)
    def _(t):
        j = peer(t, 1)
        send_k(j, me).start()
        send_v(j, me).start()

    started = []

    def part(ref, half):
        return ref.at[pl.ds(half * GROUP // 2, GROUP // 2)]

    def pass_on(shard, half, name, own=False):
        copy = pltpu.make_async_remote_copy(
            src_ref=part(w if own else w_all.at[shard], half), dst_ref=part(w_all.at[shard], half),
            send_sem=w_ss.at[len(started)], recv_sem=w_rs.at[shard, half],
            device_id=beside[name], device_id_type=MESH)
        copy.start()
        started.append(copy)

    def arrive(shard, half):
        pltpu.make_async_remote_copy(
            src_ref=part(w_all.at[shard], half), dst_ref=part(w_all.at[shard], half),
            send_sem=w_ss.at[0], recv_sem=w_rs.at[shard, half],
            device_id=beside["kin"], device_id_type=MESH).wait_recv()

    pass_on(fs, 0, "near", True)
    pass_on(fs, 1, "away", True)
    pass_on(fs, 0, "right", True)
    pass_on(fs, 1, "left", True)
    pass_on(fs, 1, "right", True)
    pass_on(fs, 0, "left", True)

    @pl.loop(1, N)
    def _(t):
        send_q(peer(t, 1), me).start()

    for half in range(2):
        pass_on(fs, half, "kin", True)

    for copy in local:
        copy.start()

    for g in range(N):
        row = docs[:, g * GROUP:(g + 1) * GROUP]
        doc_rows[g] = row.astype(jnp.float32)

    @pl.loop(0, N)
    def _(g):
        found = jnp.int32(0)
        for c in range(N):
            found = jnp.where(layout[c] == g, c, found)
        inv[g] = found

    @pl.loop(0, N)
    def _(g):
        doc_cols[g] = column_of(doc_rows[g])

    key_block = lax.broadcasted_iota(jnp.int32, (GROUP, GROUP), 0) // BLOCK
    query_block = lax.broadcasted_iota(jnp.int32, (GROUP, GROUP), 1) // BLOCK

    for copy in local[3:6]:
        copy.wait()
    mine = layout[me]
    home = (doc_cols[mine] == doc_rows[mine]) & (key_block == query_block)

    @pl.loop(0, N)
    def _(h):
        s = lax.dot_general(kn[:, lanes(h)], qn[:, lanes(h)], (((1,), (1,)), ((), ())),
                            preferred_element_type=jnp.float32)
        s = jnp.where(home, s, MASKED)
        top = jnp.max(s, axis=0, keepdims=True)
        p = jnp.exp2((s - top) * C2)
        total = jnp.sum(p, axis=0, keepdims=True)
        o = lax.dot_general(vn[:, lanes(h)], p.astype(jnp.bfloat16), (((0,), (0,)), ((), ())),
                            preferred_element_type=jnp.float32)
        o2[h] = o / total
        lse2[h] = top * C2 + jnp.log2(total)

    for copy in local[:2]:
        copy.wait()

    @pl.loop(1, N)
    def _(t):
        s = peer(t, -1)
        send_k(s, s).wait_recv()
        send_v(s, s).wait_recv()

    @pl.loop(0, N)
    def _(g):
        vt_all[g] = jnp.transpose(v_all[g].astype(jnp.float32), (1, 0)).astype(jnp.bfloat16)

    local[2].wait()

    arrive(across, 0)
    pass_on(across, 0, "right")
    pass_on(across, 0, "left")
    arrive(across, 1)
    pass_on(across, 1, "left")
    pass_on(across, 1, "right")
    arrive(left, 0)
    pass_on(left, 0, "right")
    arrive(right, 1)
    pass_on(right, 1, "left")


    def attend(t):
        d = peer(t, -1)

        @pl.when(t > 0)
        def _():
            send_q(d, d).wait_recv()

        p_q = layout[d]
        queries = q_all[d].reshape(2 * GROUP, HEAD)
        doc_q = doc_rows[p_q]
        places = []
        top = jnp.full((1, 2 * GROUP), FLOOR, jnp.float32)
        for w in range(WINDOW):
            at = (p_q - w + N) % N
            place = inv[at]
            places.append(place)
            s = lax.dot_general(k_all[place], queries, (((1,), (1,)), ((), ())),
                                preferred_element_type=jnp.float32)
            wanted = jnp.where(p_q >= w, doc_q, -1.0)
            same = doc_cols[at] == wanted
            if w == 0:
                clean = same & (key_block <= query_block)
                noisy = same & (key_block < query_block)
            else:
                clean = noisy = same
            s = jnp.concatenate([jnp.where(clean, s[:, :GROUP], MASKED), jnp.where(noisy, s[:, GROUP:], MASKED)], axis=1)
            scores[w] = s
            top = jnp.maximum(top, jnp.max(s, axis=0, keepdims=True))
        total = jnp.zeros((1, 2 * GROUP), jnp.float32)
        o = jnp.zeros((HEAD, 2 * GROUP), jnp.float32)
        for w in range(WINDOW):
            p = jnp.exp2((scores[w] - top) * C2)
            total = total + jnp.sum(p, axis=0, keepdims=True)
            o = o + jnp.dot(vt_all[places[w]], p.astype(jnp.bfloat16), preferred_element_type=jnp.float32)
        safe = jnp.maximum(total, TINY)
        o_snd[d] = (o / safe).astype(jnp.bfloat16)
        lse_snd[d] = jnp.broadcast_to(top * C2 + jnp.log2(safe), (8, 2 * GROUP))

        @pl.when(t > 0)
        def _():
            send_o(d, me).start()
            send_l(d, me).start()

        @pl.when(t == 0)
        def _():
            o_rcv[me] = o_snd[d]
            lse_rcv[me] = lse_snd[d]

    @pl.loop(0, N // 2)
    def _(t):
        attend(t)

    for half in range(2):
        pass_on(across, half, "kin")
    arrive(far, 0)
    pass_on(far, 0, "near")
    arrive(far, 1)
    pass_on(far, 1, "away")
    arrive(left, 1)
    arrive(right, 0)
    for half in range(2):
        pass_on(left, half, "kin")
        pass_on(right, half, "kin")
        pass_on(far, half, "kin")

    @pl.loop(N // 2, N)
    def _(t):
        attend(t)

    for shard in ((across + 4) % N, (across + 12) % N, (across + 8) % N):
        for half in range(2):
            arrive(shard, half)
            pass_on(shard, half, "kin")

    @pl.loop(0, N)
    def _(t):
        h = peer(t, -1)

        @pl.when(t > 0)
        def _():
            send_o(h, h).wait_recv()
            send_l(h, h).wait_recv()

        lse1 = lse_rcv[h][0:1, GROUP:]
        lse_n = lse2[h]
        high = jnp.maximum(lse1, lse_n)
        e1 = jnp.exp2(lse1 - high)
        e2 = jnp.exp2(lse_n - high)
        both = e1 + e2
        clean = o_rcv[h][:, :GROUP].astype(jnp.float32)
        noisy = o_rcv[h][:, GROUP:].astype(jnp.float32) * (e1 / both) + o2[h] * (e2 / both)
        ctx[:GROUP, lanes(h)] = jnp.transpose(clean, (1, 0)).astype(jnp.bfloat16)
        ctx[GROUP:, lanes(h)] = jnp.transpose(noisy, (1, 0)).astype(jnp.bfloat16)

    local[6].wait()
    for x in range(N // 4):
        for y in range(2):
            for half in range(2):
                arrive(x * 4 + y * 2 + (fs + 1) % 2, half)

    @pl.loop(0, w.shape[1] // TILE)
    def _(n):
        tile = pl.ds(pl.multiple_of(n * TILE, TILE), TILE)
        rows = w_all[:, :, tile].reshape(N * HEAD, TILE)
        out[:, tile] = jnp.dot(ctx[...], rows, preferred_element_type=jnp.float32).astype(jnp.bfloat16)

    @pl.loop(1, N)
    def _(t):
        j = peer(t, 1)
        send_k(j, me).wait_send()
        send_v(j, me).wait_send()
        send_q(j, me).wait_send()
        send_o(j, me).wait_send()
        send_l(j, me).wait_send()

    for copy in started:
        copy.wait_send()


def local(queries, keys, values, docs, layout, w_out):
    vm = lambda *shape: pltpu.VMEM(shape, jnp.bfloat16)
    vf = lambda *shape: pltpu.VMEM(shape, jnp.float32)
    sems = [pltpu.SemaphoreType.DMA((N,))] * 10
    any_spec = pl.BlockSpec(memory_space=pltpu.HBM)
    mixed = pl.pallas_call(
        kernel,
        out_shape=jax.ShapeDtypeStruct((2 * GROUP, w_out.shape[1]), jnp.bfloat16),
        in_specs=[
            pl.BlockSpec(memory_space=pltpu.SMEM),
            pl.BlockSpec(memory_space=pltpu.VMEM),
            any_spec, any_spec, any_spec, any_spec,
        ],
        out_specs=pl.BlockSpec(memory_space=pltpu.VMEM),
        scratch_shapes=[
            vm(N, HEAD, w_out.shape[1]), vm(2 * GROUP, N * HEAD),
            vm(N, 2, GROUP, HEAD), vm(N, GROUP, HEAD), vm(N, GROUP, HEAD), vm(N, HEAD, GROUP),
            vm(N, HEAD, 2 * GROUP), vf(N, 8, 2 * GROUP), vm(N, HEAD, 2 * GROUP), vf(N, 8, 2 * GROUP),
            vm(GROUP, N * HEAD), vm(GROUP, N * HEAD), vm(GROUP, N * HEAD),
            vf(N, HEAD, GROUP), vf(N, 1, GROUP), vf(N, 1, GROUP), vf(N, GROUP, GROUP),
            vf(WINDOW, GROUP, 2 * GROUP), pltpu.SMEM((N,), jnp.int32),
            *sems, pltpu.SemaphoreType.DMA((7,)), pltpu.SemaphoreType.DMA((30,)), pltpu.SemaphoreType.DMA((N, 2)),
        ],
        compiler_params=pltpu.CompilerParams(
            collective_id=0, has_side_effects=True, vmem_limit_bytes=60 * 2 ** 20),
        cost_estimate=pl.CostEstimate(flops=8 * 10 ** 9, bytes_accessed=8 * 10 ** 6, transcendentals=5 * 10 ** 6),
    )(layout, docs, queries, keys, values, w_out)
    return mixed.reshape(1, 2, GROUP, w_out.shape[1])


def solution(mesh):
    return jax.shard_map(
        local,
        mesh=mesh,
        in_specs=(
            P("fsdp", None, "ctx", None),
            P("fsdp", None, "ctx", None),
            P("fsdp", None, "ctx", None),
            P("fsdp", None),
            P(),
            P("fsdp", None),
        ),
        out_specs=P("fsdp", None, "ctx", None),
        check_vma=False,
    )
```

```python
import math

import jax
import jax.numpy as jnp
from jax import lax
from jax.experimental import pallas as pl
from jax.experimental.pallas import tpu as pltpu
from jax.sharding import PartitionSpec as P

MESH = pl.DeviceIdType.MESH
HEAD = 128
GROUP = 128
BLOCK = 16
HEADS = 16
N = 16
Z = 8
PAIR = 2 * HEAD
WINDOW = 1024 // GROUP + 1
MASKED = -1e30
FLOOR = -1e20
TINY = 1e-30
C2 = math.log2(math.e) / math.sqrt(HEAD)
TILE = 512


def shift(step):
    return ((step + 1) // 2) * (1 - 2 * ((step + 1) % 2))


def peer(step, sign):
    return (lax.axis_index("ctx") // 2 + sign * shift(step) + Z) % Z


def column_of(row):
    return jnp.transpose(jnp.broadcast_to(row, (GROUP, row.shape[1])), (1, 0))


def kernel(
    layout_hbm, docs_hbm, q, k, v, w, out,
    layout, docs, w_all, ctx, acc, q_all, kv_all, vt_all, o_snd, lse_snd, o_rcv, lse_rcv,
    qn, kn, vn, o2, lse2, doc_rows, doc_cols, scores, inv,
    kv_ss, kv_rs, tw_ss, q_ss, q_rs, o_ss, o_rs, l_ss, l_rs, loc, w_ss, w_rs,
):
    me = lax.axis_index("ctx")
    fs = lax.axis_index("fsdp")
    z, yh = me // 2, me % 2
    twin = z * 2 + (yh + 1) % 2
    kin = (fs // 2) * 2 + (fs + 1) % 2
    across = (fs // 4) * 4 + (fs + 2) % 4
    right, left, far = (fs + 4) % N, (fs + 12) % N, (fs + 8) % N
    beside = {"kin": (me, kin), "right": (me, right), "left": (me, left), "near": (me, across), "away": (twin, across)}

    def pair(i):
        return pl.ds(pl.multiple_of(i * PAIR, PAIR), PAIR)

    def lanes(h):
        return pl.ds(pl.multiple_of(h * HEAD, HEAD), HEAD)

    def place(zz):
        return zz * 2 + yh

    barrier = pltpu.get_barrier_semaphore()
    for name in beside:
        pl.semaphore_signal(barrier, inc=1, device_id=beside[name], device_id_type=MESH)
    pl.semaphore_signal(barrier, inc=1, device_id=(twin, fs), device_id_type=MESH)
    for t in range(1, Z):
        pl.semaphore_signal(barrier, inc=1, device_id=(place(peer(t, 1)), fs), device_id_type=MESH)

    local = [
        pltpu.make_async_copy(k.at[0, 0, :, pair(z)], kv_all.at[me, 0], loc.at[0]),
        pltpu.make_async_copy(v.at[0, 0, :, pair(z)], kv_all.at[me, 1], loc.at[1]),
        pltpu.make_async_copy(q.at[0, :, :, pair(z)], q_all.at[z], loc.at[2]),
        pltpu.make_async_copy(q.at[0, 1], qn, loc.at[3]),
        pltpu.make_async_copy(k.at[0, 1], kn, loc.at[4]),
        pltpu.make_async_copy(v.at[0, 1], vn, loc.at[5]),
        pltpu.make_async_copy(w, w_all.at[fs], loc.at[6]),
        pltpu.make_async_copy(docs_hbm, docs, loc.at[7]),
        pltpu.make_async_copy(layout_hbm, layout, loc.at[8]),
    ]
    for i in (7, 8, 3, 4, 5, 0, 1, 2, 6):
        local[i].start()
    pl.semaphore_wait(barrier, Z + len(beside))

    def send_k(j, s):
        return pltpu.make_async_remote_copy(
            src_ref=k.at[0, 0, :, pair(j)], dst_ref=kv_all.at[place(s), 0], send_sem=kv_ss.at[j, 0],
            recv_sem=kv_rs.at[place(s), 0], device_id=(place(j), fs), device_id_type=MESH)

    def send_v(j, s):
        return pltpu.make_async_remote_copy(
            src_ref=v.at[0, 0, :, pair(j)], dst_ref=kv_all.at[place(s), 1], send_sem=kv_ss.at[j, 1],
            recv_sem=kv_rs.at[place(s), 1], device_id=(place(j), fs), device_id_type=MESH)

    def send_twin(s):
        return pltpu.make_async_remote_copy(
            src_ref=kv_all.at[place(s)], dst_ref=kv_all.at[place(s)], send_sem=tw_ss.at[s],
            recv_sem=kv_rs.at[place(s), 0], device_id=(twin, fs), device_id_type=MESH)

    def take_twin(s):
        slot = s * 2 + (yh + 1) % 2
        return pltpu.make_async_remote_copy(
            src_ref=kv_all.at[slot], dst_ref=kv_all.at[slot], send_sem=tw_ss.at[s],
            recv_sem=kv_rs.at[slot, 0], device_id=(twin, fs), device_id_type=MESH)

    def send_q(j, s):
        return pltpu.make_async_remote_copy(
            src_ref=q.at[0, :, :, pair(j)], dst_ref=q_all.at[s], send_sem=q_ss.at[j],
            recv_sem=q_rs.at[s], device_id=(place(j), fs), device_id_type=MESH)

    def send_o(j, s):
        return pltpu.make_async_remote_copy(
            src_ref=o_snd.at[j], dst_ref=o_rcv.at[s], send_sem=o_ss.at[j],
            recv_sem=o_rs.at[s], device_id=(place(j), fs), device_id_type=MESH)

    def send_l(j, s):
        return pltpu.make_async_remote_copy(
            src_ref=lse_snd.at[j], dst_ref=lse_rcv.at[s], send_sem=l_ss.at[j],
            recv_sem=l_rs.at[s], device_id=(place(j), fs), device_id_type=MESH)

    started = []

    def part(ref, half):
        return ref.at[pl.ds(half * GROUP // 2, GROUP // 2)]

    def pass_on(shard, half, name, own=False):
        copy = pltpu.make_async_remote_copy(
            src_ref=part(w if own else w_all.at[shard], half), dst_ref=part(w_all.at[shard], half),
            send_sem=w_ss.at[len(started)], recv_sem=w_rs.at[shard, half],
            device_id=beside[name], device_id_type=MESH)
        copy.start()
        started.append(copy)

    def arrive(shard, half):
        pltpu.make_async_remote_copy(
            src_ref=part(w_all.at[shard], half), dst_ref=part(w_all.at[shard], half),
            send_sem=w_ss.at[0], recv_sem=w_rs.at[shard, half],
            device_id=beside["kin"], device_id_type=MESH).wait_recv()

    @pl.loop(1, Z)
    def _(t):
        j = peer(t, 1)
        send_k(j, z).start()
        send_v(j, z).start()

    pass_on(fs, 0, "near", True)
    pass_on(fs, 1, "away", True)
    pass_on(fs, 0, "right", True)
    pass_on(fs, 1, "left", True)
    local[0].wait()
    local[1].wait()
    send_twin(z).start()
    pass_on(fs, 1, "right", True)
    pass_on(fs, 0, "left", True)

    @pl.loop(1, Z)
    def _(t):
        send_q(peer(t, 1), z).start()

    for half in range(2):
        pass_on(fs, half, "kin", True)

    local[7].wait()
    local[8].wait()
    for g in range(N):
        doc_rows[g] = docs[:, g * GROUP:(g + 1) * GROUP].astype(jnp.float32)

    @pl.loop(0, N)
    def _(g):
        found = jnp.int32(0)
        for c in range(N):
            found = jnp.where(layout[c] == g, c, found)
        inv[g] = found

    @pl.loop(0, N)
    def _(g):
        doc_cols[g] = column_of(doc_rows[g])

    key_block = lax.broadcasted_iota(jnp.int32, (GROUP, GROUP), 0) // BLOCK
    query_block = lax.broadcasted_iota(jnp.int32, (GROUP, GROUP), 1) // BLOCK

    for copy in local[3:6]:
        copy.wait()
    mine = layout[me]
    home = (doc_cols[mine] == doc_rows[mine]) & (key_block == query_block)

    @pl.loop(0, HEADS)
    def _(h):
        s = lax.dot_general(kn[:, lanes(h)], qn[:, lanes(h)], (((1,), (1,)), ((), ())),
                            preferred_element_type=jnp.float32)
        s = jnp.where(home, s, MASKED)
        top = jnp.max(s, axis=0, keepdims=True)
        p = jnp.exp2((s - top) * C2)
        total = jnp.sum(p, axis=0, keepdims=True)
        o = lax.dot_general(vn[:, lanes(h)], p.astype(jnp.bfloat16), (((0,), (0,)), ((), ())),
                            preferred_element_type=jnp.float32)
        o2[h] = o / total
        lse2[h] = top * C2 + jnp.log2(total)

    def relay(low, high):
        @pl.loop(low, high)
        def _(t):
            s = peer(t, -1)
            send_k(s, s).wait_recv()
            send_v(s, s).wait_recv()
            send_twin(s).start()

    relay(1, 3)
    arrive(left, 0)
    pass_on(left, 0, "right")
    arrive(right, 1)
    pass_on(right, 1, "left")
    relay(3, 5)
    arrive(across, 0)
    pass_on(across, 0, "right")
    pass_on(across, 0, "left")
    arrive(across, 1)
    pass_on(across, 1, "left")
    pass_on(across, 1, "right")
    relay(5, Z)

    def turn(g):
        vt_all[g] = jnp.transpose(kv_all[g, 1].astype(jnp.float32), (1, 0)).astype(jnp.bfloat16)

    @pl.loop(0, Z)
    def _(zz):
        turn(place(zz))

    @pl.loop(0, Z)
    def _(t):
        s = peer(t, -1)
        take_twin(s).wait_recv()
        turn(s * 2 + (yh + 1) % 2)

    local[2].wait()

    def attend(t):
        s_z = peer(t, -1)

        @pl.when(t > 0)
        def _():
            send_q(s_z, s_z).wait_recv()

        p_q = layout[place(s_z)]
        doc_q = doc_rows[p_q]
        tops = [jnp.full((1, 2 * GROUP), FLOOR, jnp.float32)] * 2
        queries = [q_all[s_z, :, :, a * HEAD:(a + 1) * HEAD].reshape(2 * GROUP, HEAD) for a in range(2)]
        places = []
        for w_ in range(WINDOW):
            at = (p_q - w_ + N) % N
            where = inv[at]
            places.append(where)
            wanted = jnp.where(p_q >= w_, doc_q, -1.0)
            same = doc_cols[at] == wanted
            if w_ == 0:
                clean = same & (key_block <= query_block)
                noisy = same & (key_block < query_block)
            else:
                clean = noisy = same
            for a in range(2):
                s = lax.dot_general(kv_all[where, 0, :, a * HEAD:(a + 1) * HEAD], queries[a],
                                    (((1,), (1,)), ((), ())), preferred_element_type=jnp.float32)
                s = jnp.concatenate(
                    [jnp.where(clean, s[:, :GROUP], MASKED), jnp.where(noisy, s[:, GROUP:], MASKED)], axis=1)
                scores[a, w_] = s
                tops[a] = jnp.maximum(tops[a], jnp.max(s, axis=0, keepdims=True))
        for a in range(2):
            top = tops[a]
            total = jnp.zeros((1, 2 * GROUP), jnp.float32)
            o = jnp.zeros((HEAD, 2 * GROUP), jnp.float32)
            for w_ in range(WINDOW):
                p = jnp.exp2((scores[a, w_] - top) * C2)
                total = total + jnp.sum(p, axis=0, keepdims=True)
                o = o + jnp.dot(vt_all[places[w_], a * HEAD:(a + 1) * HEAD], p.astype(jnp.bfloat16),
                                preferred_element_type=jnp.float32)
            safe = jnp.maximum(total, TINY)
            o_snd[s_z, a] = (o / safe).astype(jnp.bfloat16)
            lse = top * C2 + jnp.log2(safe)
            lse_snd[s_z, a:a + 1] = lse[:, GROUP:]

        @pl.when(t > 0)
        def _():
            send_o(s_z, z).start()
            send_l(s_z, z).start()

        @pl.when(t == 0)
        def _():
            o_rcv[z] = o_snd[s_z]
            lse_rcv[z] = lse_snd[s_z]

    @pl.loop(0, Z // 2)
    def _(t):
        attend(t)

    for half in range(2):
        pass_on(across, half, "kin")
    arrive(far, 0)
    pass_on(far, 0, "near")
    arrive(far, 1)
    pass_on(far, 1, "away")
    arrive(left, 1)
    arrive(right, 0)
    for half in range(2):
        pass_on(left, half, "kin")
        pass_on(right, half, "kin")
        pass_on(far, half, "kin")

    @pl.loop(Z // 2, Z)
    def _(t):
        attend(t)

    for shard in ((across + 4) % N, (across + 12) % N, (across + 8) % N):
        for half in range(2):
            arrive(shard, half)
            pass_on(shard, half, "kin")

    def merge(t):
        s_z = peer(t, -1)
        if t > 0:
            send_o(s_z, s_z).wait_recv()
            send_l(s_z, s_z).wait_recv()
        for a in range(2):
            lse1 = lse_rcv[s_z, a:a + 1]
            lse_n = lse2[s_z * 2 + a]
            high = jnp.maximum(lse1, lse_n)
            e1 = jnp.exp2(lse1 - high)
            e2 = jnp.exp2(lse_n - high)
            both = e1 + e2
            o1 = o_rcv[s_z, a].astype(jnp.float32)
            noisy = o1[:, GROUP:] * (e1 / both) + o2[s_z * 2 + a] * (e2 / both)
            side = slice(a * HEAD, (a + 1) * HEAD)
            ctx[s_z, :GROUP, side] = jnp.transpose(o1[:, :GROUP], (1, 0)).astype(jnp.bfloat16)
            ctx[s_z, GROUP:, side] = jnp.transpose(noisy, (1, 0)).astype(jnp.bfloat16)

    def project(steps, first, last):
        @pl.loop(0, w.shape[1] // TILE)
        def _(n):
            tile = pl.ds(pl.multiple_of(n * TILE, TILE), TILE)
            total = None if first else acc[:, tile]
            for t in steps:
                s_z = peer(t, -1)
                rows = w_all[pl.ds(s_z * 2, 2), :, tile].reshape(PAIR, TILE)
                term = jnp.dot(ctx[s_z], rows, preferred_element_type=jnp.float32)
                total = term if total is None else total + term
            if last:
                out[:, tile] = total.astype(jnp.bfloat16)
            else:
                acc[:, tile] = total

    for t in range(4):
        merge(t)
    local[6].wait()
    for i in range(HEADS // 2):
        for half in range(2):
            arrive(i * 2 + (fs + 1) % 2, half)
    project((0, 1, 2, 3), True, False)
    merge(4)
    merge(5)
    project((4, 5), False, False)
    merge(6)
    merge(7)
    project((6, 7), False, True)

    @pl.loop(0, Z)
    def _(s):
        send_twin(s).wait_send()

    @pl.loop(1, Z)
    def _(t):
        j = peer(t, 1)
        send_k(j, z).wait_send()
        send_v(j, z).wait_send()
        send_q(j, z).wait_send()
        send_o(j, z).wait_send()
        send_l(j, z).wait_send()

    for copy in started:
        copy.wait_send()


def local(queries, keys, values, docs, layout, w_out):
    def vm(*shape):
        return pltpu.VMEM(shape, jnp.bfloat16)

    def vf(*shape):
        return pltpu.VMEM(shape, jnp.float32)

    def dma(*shape):
        return pltpu.SemaphoreType.DMA(shape)

    width = w_out.shape[1]
    operands = [pltpu.with_memory_space_constraint(a, pltpu.HBM) for a in (layout, docs, queries, keys, values, w_out)]
    mixed = pl.pallas_call(
        kernel,
        out_shape=jax.ShapeDtypeStruct((2 * GROUP, width), jnp.bfloat16),
        in_specs=[pl.BlockSpec(memory_space=pltpu.HBM)] * 6,
        out_specs=pl.BlockSpec(memory_space=pltpu.VMEM),
        scratch_shapes=[
            pltpu.SMEM((N,), jnp.int32), pltpu.VMEM((1, N * GROUP), jnp.int32),
            vm(HEADS, HEAD, width), vm(Z, 2 * GROUP, PAIR), vf(2 * GROUP, width),
            vm(Z, 2, GROUP, PAIR), vm(N, 2, GROUP, PAIR), vm(N, PAIR, GROUP),
            vm(Z, 2, HEAD, 2 * GROUP), vf(Z, 8, GROUP), vm(Z, 2, HEAD, 2 * GROUP), vf(Z, 8, GROUP),
            vm(GROUP, HEADS * HEAD), vm(GROUP, HEADS * HEAD), vm(GROUP, HEADS * HEAD),
            vf(HEADS, HEAD, GROUP), vf(HEADS, 1, GROUP), vf(N, 1, GROUP), vf(N, GROUP, GROUP),
            vf(2, WINDOW, GROUP, 2 * GROUP), pltpu.SMEM((N,), jnp.int32),
            dma(Z, 2), dma(N, 2), dma(Z), dma(Z), dma(Z), dma(Z), dma(Z), dma(Z), dma(Z),
            dma(9), dma(30), dma(HEADS, 2),
        ],
        compiler_params=pltpu.CompilerParams(
            collective_id=0, has_side_effects=True, vmem_limit_bytes=48 * 2 ** 20),
        cost_estimate=pl.CostEstimate(flops=8 * 10 ** 9, bytes_accessed=8 * 10 ** 6, transcendentals=5 * 10 ** 6),
    )(*operands)
    return mixed.reshape(1, 2, GROUP, width)


def solution(mesh):
    return jax.shard_map(
        local,
        mesh=mesh,
        in_specs=(
            P("fsdp", None, "ctx", None),
            P("fsdp", None, "ctx", None),
            P("fsdp", None, "ctx", None),
            P("fsdp", None),
            P(),
            P("fsdp", None),
        ),
        out_specs=P("fsdp", None, "ctx", None),
        check_vma=False,
    )
```

```python
import math

import jax
import jax.numpy as jnp
from jax import lax
from jax.experimental import pallas as pl
from jax.experimental.pallas import tpu as pltpu
from jax.sharding import PartitionSpec as P

MESH = pl.DeviceIdType.MESH
HEAD = 128
GROUP = 128
BLOCK = 16
HEADS = 16
N = 16
Z = 8
PAIR = 2 * HEAD
WINDOW = 1024 // GROUP + 1
MASKED = -1e30
FLOOR = -1e20
TINY = 1e-30
C2 = math.log2(math.e) / math.sqrt(HEAD)
TILE = 2048


def shift(step):
    back = (Z - step) % Z
    return ((back + 1) // 2) * (1 - 2 * ((back + 1) % 2))


def peer(step, sign):
    return (lax.axis_index("ctx") // 2 + sign * shift(step) + Z) % Z


def column_of(row):
    return jnp.transpose(jnp.broadcast_to(row, (GROUP, row.shape[1])), (1, 0))


def kernel(
    layout_hbm, docs_hbm, q, k, v, w, out,
    layout, docs, w_all, ctx, acc, q_all, kv_all, vt_all, o_snd, lse_snd, o_rcv, lse_rcv,
    qn, kn, vn, o2, lse2, doc_rows, doc_cols, scores, inv,
    kv_ss, kv_rs, tw_ss, q_ss, q_rs, o_ss, o_rs, l_ss, l_rs, loc, w_ss, w_rs,
):
    me = lax.axis_index("ctx")
    fs = lax.axis_index("fsdp")
    z, yh = me // 2, me % 2
    twin = z * 2 + (yh + 1) % 2
    kin = (fs // 2) * 2 + (fs + 1) % 2
    across = (fs // 4) * 4 + (fs + 2) % 4
    right, left, far = (fs + 4) % N, (fs + 12) % N, (fs + 8) % N
    beside = {"kin": (me, kin), "right": (me, right), "left": (me, left), "near": (me, across), "away": (twin, across)}

    def pair(i):
        return pl.ds(pl.multiple_of(i * PAIR, PAIR), PAIR)

    def lanes(h):
        return pl.ds(pl.multiple_of(h * HEAD, HEAD), HEAD)

    def place(zz):
        return zz * 2 + yh

    barrier = pltpu.get_barrier_semaphore()
    for name in beside:
        pl.semaphore_signal(barrier, inc=1, device_id=beside[name], device_id_type=MESH)
    pl.semaphore_signal(barrier, inc=1, device_id=(twin, fs), device_id_type=MESH)
    for t in range(1, Z):
        pl.semaphore_signal(barrier, inc=1, device_id=(place(peer(t, 1)), fs), device_id_type=MESH)

    local = [
        pltpu.make_async_copy(k.at[0, 0, :, pair(z)], kv_all.at[me, 0], loc.at[0]),
        pltpu.make_async_copy(v.at[0, 0, :, pair(z)], kv_all.at[me, 1], loc.at[1]),
        pltpu.make_async_copy(q.at[0, :, :, pair(z)], q_all.at[z], loc.at[2]),
        pltpu.make_async_copy(q.at[0, 1], qn, loc.at[3]),
        pltpu.make_async_copy(k.at[0, 1], kn, loc.at[4]),
        pltpu.make_async_copy(v.at[0, 1], vn, loc.at[5]),
        pltpu.make_async_copy(w, w_all.at[fs], loc.at[6]),
        pltpu.make_async_copy(docs_hbm, docs, loc.at[7]),
        pltpu.make_async_copy(layout_hbm, layout, loc.at[8]),
    ]
    for i in (7, 8, 3, 4, 5, 0, 1, 2, 6):
        local[i].start()
    pl.semaphore_wait(barrier, Z + len(beside))

    def send_k(j, s):
        return pltpu.make_async_remote_copy(
            src_ref=k.at[0, 0, :, pair(j)], dst_ref=kv_all.at[place(s), 0], send_sem=kv_ss.at[j, 0],
            recv_sem=kv_rs.at[place(s), 0], device_id=(place(j), fs), device_id_type=MESH)

    def send_v(j, s):
        return pltpu.make_async_remote_copy(
            src_ref=v.at[0, 0, :, pair(j)], dst_ref=kv_all.at[place(s), 1], send_sem=kv_ss.at[j, 1],
            recv_sem=kv_rs.at[place(s), 1], device_id=(place(j), fs), device_id_type=MESH)

    def send_twin(s):
        return pltpu.make_async_remote_copy(
            src_ref=kv_all.at[place(s)], dst_ref=kv_all.at[place(s)], send_sem=tw_ss.at[s],
            recv_sem=kv_rs.at[place(s), 0], device_id=(twin, fs), device_id_type=MESH)

    def take_twin(s):
        slot = s * 2 + (yh + 1) % 2
        return pltpu.make_async_remote_copy(
            src_ref=kv_all.at[slot], dst_ref=kv_all.at[slot], send_sem=tw_ss.at[s],
            recv_sem=kv_rs.at[slot, 0], device_id=(twin, fs), device_id_type=MESH)

    def send_q(j, s):
        return pltpu.make_async_remote_copy(
            src_ref=q.at[0, :, :, pair(j)], dst_ref=q_all.at[s], send_sem=q_ss.at[j],
            recv_sem=q_rs.at[s], device_id=(place(j), fs), device_id_type=MESH)

    def send_o(j, s):
        return pltpu.make_async_remote_copy(
            src_ref=o_snd.at[j], dst_ref=o_rcv.at[s], send_sem=o_ss.at[j],
            recv_sem=o_rs.at[s], device_id=(place(j), fs), device_id_type=MESH)

    def send_l(j, s):
        return pltpu.make_async_remote_copy(
            src_ref=lse_snd.at[j], dst_ref=lse_rcv.at[s], send_sem=l_ss.at[j],
            recv_sem=l_rs.at[s], device_id=(place(j), fs), device_id_type=MESH)

    started = []

    def part(ref, half):
        return ref.at[pl.ds(half * GROUP // 2, GROUP // 2)]

    def pass_on(shard, half, name, own=False):
        copy = pltpu.make_async_remote_copy(
            src_ref=part(w if own else w_all.at[shard], half), dst_ref=part(w_all.at[shard], half),
            send_sem=w_ss.at[len(started)], recv_sem=w_rs.at[shard, half],
            device_id=beside[name], device_id_type=MESH)
        copy.start()
        started.append(copy)

    def arrive(shard, half):
        pltpu.make_async_remote_copy(
            src_ref=part(w_all.at[shard], half), dst_ref=part(w_all.at[shard], half),
            send_sem=w_ss.at[0], recv_sem=w_rs.at[shard, half],
            device_id=beside["kin"], device_id_type=MESH).wait_recv()

    @pl.loop(1, Z)
    def _(t):
        j = peer(t, 1)
        send_k(j, z).start()
        send_v(j, z).start()

    pass_on(fs, 0, "near", True)
    pass_on(fs, 1, "away", True)
    pass_on(fs, 0, "right", True)
    pass_on(fs, 1, "left", True)
    local[0].wait()
    local[1].wait()
    send_twin(z).start()
    pass_on(fs, 1, "right", True)
    pass_on(fs, 0, "left", True)

    @pl.loop(1, Z)
    def _(t):
        send_q(peer(t, 1), z).start()

    for half in range(2):
        pass_on(fs, half, "kin", True)

    local[7].wait()
    local[8].wait()
    for g in range(N):
        doc_rows[g] = docs[:, g * GROUP:(g + 1) * GROUP].astype(jnp.float32)

    @pl.loop(0, N)
    def _(g):
        found = jnp.int32(0)
        for c in range(N):
            found = jnp.where(layout[c] == g, c, found)
        inv[g] = found

    @pl.loop(0, N)
    def _(g):
        doc_cols[g] = column_of(doc_rows[g])

    key_block = lax.broadcasted_iota(jnp.int32, (GROUP, GROUP), 0) // BLOCK
    query_block = lax.broadcasted_iota(jnp.int32, (GROUP, GROUP), 1) // BLOCK

    for copy in local[3:6]:
        copy.wait()
    mine = layout[me]
    home = (doc_cols[mine] == doc_rows[mine]) & (key_block == query_block)

    @pl.loop(0, HEADS)
    def _(h):
        s = lax.dot_general(kn[:, lanes(h)], qn[:, lanes(h)], (((1,), (1,)), ((), ())),
                            preferred_element_type=jnp.float32)
        s = jnp.where(home, s, MASKED)
        top = jnp.max(s, axis=0, keepdims=True)
        p = jnp.exp2((s - top) * C2)
        total = jnp.sum(p, axis=0, keepdims=True)
        o = lax.dot_general(vn[:, lanes(h)], p.astype(jnp.bfloat16), (((0,), (0,)), ((), ())),
                            preferred_element_type=jnp.float32)
        o2[h] = o / total
        lse2[h] = top * C2 + jnp.log2(total)

    def relay(low, high):
        @pl.loop(low, high)
        def _(t):
            s = peer(t, -1)
            send_k(s, s).wait_recv()
            send_v(s, s).wait_recv()
            send_twin(s).start()

    relay(1, 3)
    arrive(left, 0)
    pass_on(left, 0, "right")
    arrive(right, 1)
    pass_on(right, 1, "left")
    relay(3, 5)
    arrive(across, 0)
    pass_on(across, 0, "right")
    arrive(across, 1)
    pass_on(across, 1, "left")
    pass_on(left, 0, "kin")
    pass_on(right, 1, "kin")
    relay(5, Z)
    arrive(left, 1)
    pass_on(left, 1, "away")
    arrive(right, 0)
    pass_on(right, 0, "near")
    pass_on(left, 1, "kin")
    pass_on(right, 0, "kin")
    for half in range(2):
        pass_on(across, half, "kin")

    def turn(g):
        vt_all[g] = jnp.transpose(kv_all[g, 1].astype(jnp.float32), (1, 0)).astype(jnp.bfloat16)

    @pl.loop(0, Z)
    def _(zz):
        turn(place(zz))

    @pl.loop(0, Z)
    def _(t):
        s = peer(t, -1)
        take_twin(s).wait_recv()
        turn(s * 2 + (yh + 1) % 2)

    local[2].wait()

    def attend(t):
        s_z = peer(t, -1)

        @pl.when(t > 0)
        def _():
            send_q(s_z, s_z).wait_recv()

        p_q = layout[place(s_z)]
        doc_q = doc_rows[p_q]
        tops = [jnp.full((1, 2 * GROUP), FLOOR, jnp.float32)] * 2
        queries = [q_all[s_z, :, :, a * HEAD:(a + 1) * HEAD].reshape(2 * GROUP, HEAD) for a in range(2)]
        places = []
        for w_ in range(WINDOW):
            at = (p_q - w_ + N) % N
            where = inv[at]
            places.append(where)
            wanted = jnp.where(p_q >= w_, doc_q, -1.0)
            same = doc_cols[at] == wanted
            if w_ == 0:
                clean = same & (key_block <= query_block)
                noisy = same & (key_block < query_block)
            else:
                clean = noisy = same
            for a in range(2):
                s = lax.dot_general(kv_all[where, 0, :, a * HEAD:(a + 1) * HEAD], queries[a],
                                    (((1,), (1,)), ((), ())), preferred_element_type=jnp.float32)
                s = jnp.concatenate(
                    [jnp.where(clean, s[:, :GROUP], MASKED), jnp.where(noisy, s[:, GROUP:], MASKED)], axis=1)
                scores[a, w_] = s
                tops[a] = jnp.maximum(tops[a], jnp.max(s, axis=0, keepdims=True))
        for a in range(2):
            top = tops[a]
            total = jnp.zeros((1, 2 * GROUP), jnp.float32)
            o = jnp.zeros((HEAD, 2 * GROUP), jnp.float32)
            for w_ in range(WINDOW):
                p = jnp.exp2((scores[a, w_] - top) * C2)
                total = total + jnp.sum(p, axis=0, keepdims=True)
                o = o + jnp.dot(vt_all[places[w_], a * HEAD:(a + 1) * HEAD], p.astype(jnp.bfloat16),
                                preferred_element_type=jnp.float32)
            safe = jnp.maximum(total, TINY)
            o_snd[s_z, a] = (o / safe).astype(jnp.bfloat16)
            lse = top * C2 + jnp.log2(safe)
            lse_snd[s_z, a:a + 1] = lse[:, GROUP:]

        @pl.when(t > 0)
        def _():
            send_o(s_z, z).start()
            send_l(s_z, z).start()

        @pl.when(t == 0)
        def _():
            o_rcv[z] = o_snd[s_z]
            lse_rcv[z] = lse_snd[s_z]

    @pl.loop(0, Z // 2)
    def _(t):
        attend(t)

    arrive(far, 0)
    pass_on(far, 0, "near")
    arrive(far, 1)
    pass_on(far, 1, "away")
    for half in range(2):
        pass_on(far, half, "kin")

    @pl.loop(Z // 2, Z)
    def _(t):
        attend(t)

    for shard in ((across + 4) % N, (across + 12) % N, (across + 8) % N):
        for half in range(2):
            arrive(shard, half)
            pass_on(shard, half, "kin")

    def merge(t):
        s_z = peer(t, -1)
        if t > 0:
            send_o(s_z, s_z).wait_recv()
            send_l(s_z, s_z).wait_recv()
        for a in range(2):
            lse1 = lse_rcv[s_z, a:a + 1]
            lse_n = lse2[s_z * 2 + a]
            high = jnp.maximum(lse1, lse_n)
            e1 = jnp.exp2(lse1 - high)
            e2 = jnp.exp2(lse_n - high)
            both = e1 + e2
            o1 = o_rcv[s_z, a].astype(jnp.float32)
            noisy = o1[:, GROUP:] * (e1 / both) + o2[s_z * 2 + a] * (e2 / both)
            side = slice(a * HEAD, (a + 1) * HEAD)
            ctx[s_z, :GROUP, side] = jnp.transpose(o1[:, :GROUP], (1, 0)).astype(jnp.bfloat16)
            ctx[s_z, GROUP:, side] = jnp.transpose(noisy, (1, 0)).astype(jnp.bfloat16)

    def project(steps, first, last):
        @pl.loop(0, w.shape[1] // TILE)
        def _(n):
            tile = pl.ds(pl.multiple_of(n * TILE, TILE), TILE)
            total = None if first else acc[:, tile]
            for t in steps:
                s_z = peer(t, -1)
                rows = w_all[pl.ds(s_z * 2, 2), :, tile].reshape(PAIR, TILE)
                term = jnp.dot(ctx[s_z], rows, preferred_element_type=jnp.float32)
                total = term if total is None else total + term
            if last:
                out[:, tile] = total.astype(jnp.bfloat16)
            else:
                acc[:, tile] = total

    for t in (0, 1, 2, 3):
        merge(t)
    local[6].wait()
    for i in range(HEADS // 2):
        for half in range(2):
            arrive(i * 2 + (fs + 1) % 2, half)
    project((0, 1, 2, 3), True, False)
    for t in (4, 5):
        merge(t)
    project((4, 5), False, False)
    for copy in started:
        copy.wait_send()

    @pl.loop(0, Z)
    def _(s):
        send_twin(s).wait_send()

    @pl.loop(1, Z)
    def _(t):
        j = peer(t, 1)
        send_k(j, z).wait_send()
        send_v(j, z).wait_send()
        send_q(j, z).wait_send()

    @pl.loop(1, 6)
    def _(t):
        j = peer(t, -1)
        send_o(j, z).wait_send()
        send_l(j, z).wait_send()

    for t in (6, 7):
        merge(t)
    project((6, 7), False, True)

    for t in (6, 7):
        send_o(peer(t, -1), z).wait_send()
        send_l(peer(t, -1), z).wait_send()


def local(queries, keys, values, docs, layout, w_out):
    def vm(*shape):
        return pltpu.VMEM(shape, jnp.bfloat16)

    def vf(*shape):
        return pltpu.VMEM(shape, jnp.float32)

    def dma(*shape):
        return pltpu.SemaphoreType.DMA(shape)

    width = w_out.shape[1]
    operands = [pltpu.with_memory_space_constraint(a, pltpu.HBM) for a in (layout, docs, queries, keys, values, w_out)]
    mixed = pl.pallas_call(
        kernel,
        out_shape=jax.ShapeDtypeStruct((2 * GROUP, width), jnp.bfloat16),
        in_specs=[pl.BlockSpec(memory_space=pltpu.HBM)] * 6,
        out_specs=pl.BlockSpec(memory_space=pltpu.VMEM),
        scratch_shapes=[
            pltpu.SMEM((N,), jnp.int32), pltpu.VMEM((1, N * GROUP), jnp.int32),
            vm(HEADS, HEAD, width), vm(Z, 2 * GROUP, PAIR), vf(2 * GROUP, width),
            vm(Z, 2, GROUP, PAIR), vm(N, 2, GROUP, PAIR), vm(N, PAIR, GROUP),
            vm(Z, 2, HEAD, 2 * GROUP), vf(Z, 8, GROUP), vm(Z, 2, HEAD, 2 * GROUP), vf(Z, 8, GROUP),
            vm(GROUP, HEADS * HEAD), vm(GROUP, HEADS * HEAD), vm(GROUP, HEADS * HEAD),
            vf(HEADS, HEAD, GROUP), vf(HEADS, 1, GROUP), vf(N, 1, GROUP), vf(N, GROUP, GROUP),
            vf(2, WINDOW, GROUP, 2 * GROUP), pltpu.SMEM((N,), jnp.int32),
            dma(Z, 2), dma(N, 2), dma(Z), dma(Z), dma(Z), dma(Z), dma(Z), dma(Z), dma(Z),
            dma(9), dma(30), dma(HEADS, 2),
        ],
        compiler_params=pltpu.CompilerParams(
            collective_id=0, has_side_effects=True, vmem_limit_bytes=48 * 2 ** 20),
        cost_estimate=pl.CostEstimate(flops=8 * 10 ** 9, bytes_accessed=8 * 10 ** 6, transcendentals=5 * 10 ** 6),
    )(*operands)
    return mixed.reshape(1, 2, GROUP, width)


def solution(mesh):
    return jax.shard_map(
        local,
        mesh=mesh,
        in_specs=(
            P("fsdp", None, "ctx", None),
            P("fsdp", None, "ctx", None),
            P("fsdp", None, "ctx", None),
            P("fsdp", None),
            P(),
            P("fsdp", None),
        ),
        out_specs=P("fsdp", None, "ctx", None),
        check_vma=False,
    )
```

```python
import math

import jax
import jax.numpy as jnp
from jax import lax
from jax.experimental import pallas as pl
from jax.experimental.pallas import tpu as pltpu
from jax.sharding import PartitionSpec as P

MESH = pl.DeviceIdType.MESH
HEAD = 128
GROUP = 128
BLOCK = 16
HEADS = 16
N = 16
Z = 8
PAIR = 2 * HEAD
WINDOW = 1024 // GROUP + 1
MASKED = -1e30
FLOOR = -1e20
TINY = 1e-30
C2 = math.log2(math.e) / math.sqrt(HEAD)
TILE = 2048


def shift(step):
    back = (Z - step) % Z
    return ((back + 1) // 2) * (1 - 2 * ((back + 1) % 2))


def peer(step, sign):
    return (lax.axis_index("ctx") // 2 + sign * shift(step) + Z) % Z


def column_of(row):
    return jnp.transpose(jnp.broadcast_to(row, (GROUP, row.shape[1])), (1, 0))


def kernel(
    layout_hbm, docs_hbm, q, k, v, w, out,
    layout, docs, w_all, ctx, acc, q_all, kv_all, vt_all, o_snd, lse_snd, o_rcv, lse_rcv,
    qn, kn, vn, o2, lse2, doc_rows, doc_cols, scores, inv,
    kv_ss, kv_rs, tw_ss, q_ss, q_rs, o_ss, o_rs, l_ss, l_rs, loc, w_ss, w_rs,
):
    me = lax.axis_index("ctx")
    fs = lax.axis_index("fsdp")
    z, yh = me // 2, me % 2
    twin = z * 2 + (yh + 1) % 2
    kin = (fs // 2) * 2 + (fs + 1) % 2
    across = (fs // 4) * 4 + (fs + 2) % 4
    right, left, far = (fs + 4) % N, (fs + 12) % N, (fs + 8) % N
    beside = {"kin": (me, kin), "right": (me, right), "left": (me, left), "near": (me, across), "away": (twin, across)}

    def pair(i):
        return pl.ds(pl.multiple_of(i * PAIR, PAIR), PAIR)

    def lanes(h):
        return pl.ds(pl.multiple_of(h * HEAD, HEAD), HEAD)

    def place(zz):
        return zz * 2 + yh

    barrier = pltpu.get_barrier_semaphore()
    for t in range(1, Z):
        pl.semaphore_signal(barrier, inc=1, device_id=(place(peer(t, 1)), fs), device_id_type=MESH)
    pl.semaphore_signal(barrier, inc=1, device_id=(twin, fs), device_id_type=MESH)
    for name in beside:
        pl.semaphore_signal(barrier, inc=1, device_id=beside[name], device_id_type=MESH)

    local = [
        pltpu.make_async_copy(k.at[0, 0, :, pair(z)], kv_all.at[me, 0], loc.at[0]),
        pltpu.make_async_copy(v.at[0, 0, :, pair(z)], kv_all.at[me, 1], loc.at[1]),
        pltpu.make_async_copy(q.at[0, :, :, pair(z)], q_all.at[z], loc.at[2]),
        pltpu.make_async_copy(q.at[0, 1], qn, loc.at[3]),
        pltpu.make_async_copy(k.at[0, 1], kn, loc.at[4]),
        pltpu.make_async_copy(v.at[0, 1], vn, loc.at[5]),
        pltpu.make_async_copy(w, w_all.at[fs], loc.at[6]),
        pltpu.make_async_copy(docs_hbm, docs, loc.at[7]),
        pltpu.make_async_copy(layout_hbm, layout, loc.at[8]),
    ]
    pl.semaphore_wait(barrier, Z + len(beside))

    def send_k(j, s):
        return pltpu.make_async_remote_copy(
            src_ref=k.at[0, 0, :, pair(j)], dst_ref=kv_all.at[place(s), 0], send_sem=kv_ss.at[j, 0],
            recv_sem=kv_rs.at[place(s), 0], device_id=(place(j), fs), device_id_type=MESH)

    def send_v(j, s):
        return pltpu.make_async_remote_copy(
            src_ref=v.at[0, 0, :, pair(j)], dst_ref=kv_all.at[place(s), 1], send_sem=kv_ss.at[j, 1],
            recv_sem=kv_rs.at[place(s), 1], device_id=(place(j), fs), device_id_type=MESH)

    def send_twin(s):
        return pltpu.make_async_remote_copy(
            src_ref=kv_all.at[place(s)], dst_ref=kv_all.at[place(s)], send_sem=tw_ss.at[s],
            recv_sem=kv_rs.at[place(s), 0], device_id=(twin, fs), device_id_type=MESH)

    def take_twin(s):
        slot = s * 2 + (yh + 1) % 2
        return pltpu.make_async_remote_copy(
            src_ref=kv_all.at[slot], dst_ref=kv_all.at[slot], send_sem=tw_ss.at[s],
            recv_sem=kv_rs.at[slot, 0], device_id=(twin, fs), device_id_type=MESH)

    def send_q(j, s):
        return pltpu.make_async_remote_copy(
            src_ref=q.at[0, :, :, pair(j)], dst_ref=q_all.at[s], send_sem=q_ss.at[j],
            recv_sem=q_rs.at[s], device_id=(place(j), fs), device_id_type=MESH)

    def send_o(j, s):
        return pltpu.make_async_remote_copy(
            src_ref=o_snd.at[j], dst_ref=o_rcv.at[s], send_sem=o_ss.at[j],
            recv_sem=o_rs.at[s], device_id=(place(j), fs), device_id_type=MESH)

    def send_l(j, s):
        return pltpu.make_async_remote_copy(
            src_ref=lse_snd.at[j], dst_ref=lse_rcv.at[s], send_sem=l_ss.at[j],
            recv_sem=l_rs.at[s], device_id=(place(j), fs), device_id_type=MESH)

    started = []

    def part(ref, half):
        return ref.at[pl.ds(half * GROUP // 2, GROUP // 2)]

    def pass_on(shard, half, name, own=False):
        copy = pltpu.make_async_remote_copy(
            src_ref=part(w if own else w_all.at[shard], half), dst_ref=part(w_all.at[shard], half),
            send_sem=w_ss.at[len(started)], recv_sem=w_rs.at[shard, half],
            device_id=beside[name], device_id_type=MESH)
        copy.start()
        started.append(copy)

    def arrive(shard, half):
        pltpu.make_async_remote_copy(
            src_ref=part(w_all.at[shard], half), dst_ref=part(w_all.at[shard], half),
            send_sem=w_ss.at[0], recv_sem=w_rs.at[shard, half],
            device_id=beside["kin"], device_id_type=MESH).wait_recv()

    @pl.loop(1, Z)
    def _(t):
        j = peer(t, 1)
        send_k(j, z).start()
        send_v(j, z).start()

    for i in (0, 1, 7, 8, 3, 4, 5, 2, 6):
        local[i].start()
    pass_on(fs, 0, "near", True)
    pass_on(fs, 1, "away", True)
    pass_on(fs, 0, "right", True)
    pass_on(fs, 1, "left", True)
    local[0].wait()
    local[1].wait()
    send_twin(z).start()
    pass_on(fs, 1, "right", True)
    pass_on(fs, 0, "left", True)

    @pl.loop(1, Z)
    def _(t):
        send_q(peer(t, 1), z).start()

    for half in range(2):
        pass_on(fs, half, "kin", True)

    local[7].wait()
    local[8].wait()
    for g in range(N):
        doc_rows[g] = docs[:, g * GROUP:(g + 1) * GROUP].astype(jnp.float32)

    @pl.loop(0, N)
    def _(g):
        found = jnp.int32(0)
        for c in range(N):
            found = jnp.where(layout[c] == g, c, found)
        inv[g] = found

    @pl.loop(0, N)
    def _(g):
        doc_cols[g] = column_of(doc_rows[g])

    key_block = lax.broadcasted_iota(jnp.int32, (GROUP, GROUP), 0) // BLOCK
    query_block = lax.broadcasted_iota(jnp.int32, (GROUP, GROUP), 1) // BLOCK

    for copy in local[3:6]:
        copy.wait()
    mine = layout[me]
    home = (doc_cols[mine] == doc_rows[mine]) & (key_block == query_block)

    @pl.loop(0, HEADS)
    def _(h):
        s = lax.dot_general(kn[:, lanes(h)], qn[:, lanes(h)], (((1,), (1,)), ((), ())),
                            preferred_element_type=jnp.float32)
        s = jnp.where(home, s, MASKED)
        top = jnp.max(s, axis=0, keepdims=True)
        p = jnp.exp2((s - top) * C2)
        total = jnp.sum(p, axis=0, keepdims=True)
        o = lax.dot_general(vn[:, lanes(h)], p.astype(jnp.bfloat16), (((0,), (0,)), ((), ())),
                            preferred_element_type=jnp.float32)
        o2[h] = o / total
        lse2[h] = top * C2 + jnp.log2(total)

    def relay(low, high):
        @pl.loop(low, high)
        def _(t):
            s = peer(t, -1)
            send_k(s, s).wait_recv()
            send_v(s, s).wait_recv()
            send_twin(s).start()

    relay(1, 3)
    arrive(left, 0)
    pass_on(left, 0, "right")
    arrive(right, 1)
    pass_on(right, 1, "left")
    relay(3, 5)
    arrive(across, 0)
    pass_on(across, 0, "right")
    arrive(across, 1)
    pass_on(across, 1, "left")
    pass_on(left, 0, "kin")
    pass_on(right, 1, "kin")
    relay(5, Z)
    arrive(left, 1)
    pass_on(left, 1, "away")
    arrive(right, 0)
    pass_on(right, 0, "near")
    pass_on(left, 1, "kin")
    pass_on(right, 0, "kin")
    for half in range(2):
        pass_on(across, half, "kin")

    def turn(g):
        vt_all[g] = jnp.transpose(kv_all[g, 1].astype(jnp.float32), (1, 0)).astype(jnp.bfloat16)

    @pl.loop(0, Z)
    def _(zz):
        turn(place(zz))

    @pl.loop(0, Z)
    def _(t):
        s = peer(t, -1)
        take_twin(s).wait_recv()
        turn(s * 2 + (yh + 1) % 2)

    local[2].wait()

    def attend(t):
        s_z = peer(t, -1)

        @pl.when(t > 0)
        def _():
            send_q(s_z, s_z).wait_recv()

        p_q = layout[place(s_z)]
        doc_q = doc_rows[p_q]
        tops = [jnp.full((1, 2 * GROUP), FLOOR, jnp.float32)] * 2
        queries = [q_all[s_z, :, :, a * HEAD:(a + 1) * HEAD].reshape(2 * GROUP, HEAD) for a in range(2)]
        places = []
        for w_ in range(WINDOW):
            at = (p_q - w_ + N) % N
            where = inv[at]
            places.append(where)
            wanted = jnp.where(p_q >= w_, doc_q, -1.0)
            same = doc_cols[at] == wanted
            if w_ == 0:
                clean = same & (key_block <= query_block)
                noisy = same & (key_block < query_block)
            else:
                clean = noisy = same
            for a in range(2):
                s = lax.dot_general(kv_all[where, 0, :, a * HEAD:(a + 1) * HEAD], queries[a],
                                    (((1,), (1,)), ((), ())), preferred_element_type=jnp.float32)
                s = jnp.concatenate(
                    [jnp.where(clean, s[:, :GROUP], MASKED), jnp.where(noisy, s[:, GROUP:], MASKED)], axis=1)
                scores[a, w_] = s
                tops[a] = jnp.maximum(tops[a], jnp.max(s, axis=0, keepdims=True))
        for a in range(2):
            top = tops[a]
            total = jnp.zeros((1, 2 * GROUP), jnp.float32)
            o = jnp.zeros((HEAD, 2 * GROUP), jnp.float32)
            for w_ in range(WINDOW):
                p = jnp.exp2((scores[a, w_] - top) * C2)
                total = total + jnp.sum(p, axis=0, keepdims=True)
                o = o + jnp.dot(vt_all[places[w_], a * HEAD:(a + 1) * HEAD], p.astype(jnp.bfloat16),
                                preferred_element_type=jnp.float32)
            safe = jnp.maximum(total, TINY)
            o_snd[s_z, a] = (o / safe).astype(jnp.bfloat16)
            lse = top * C2 + jnp.log2(safe)
            lse_snd[s_z, a:a + 1] = lse[:, GROUP:]

        @pl.when(t > 0)
        def _():
            send_o(s_z, z).start()
            send_l(s_z, z).start()

        @pl.when(t == 0)
        def _():
            o_rcv[z] = o_snd[s_z]
            lse_rcv[z] = lse_snd[s_z]

    @pl.loop(0, Z // 2)
    def _(t):
        attend(t)

    arrive(far, 0)
    pass_on(far, 0, "near")
    arrive(far, 1)
    pass_on(far, 1, "away")
    for half in range(2):
        pass_on(far, half, "kin")

    @pl.loop(Z // 2, Z)
    def _(t):
        attend(t)

    for shard in ((across + 4) % N, (across + 12) % N, (across + 8) % N):
        for half in range(2):
            arrive(shard, half)
            pass_on(shard, half, "kin")

    def merge(t):
        s_z = peer(t, -1)
        if t > 0:
            send_o(s_z, s_z).wait_recv()
            send_l(s_z, s_z).wait_recv()
        for a in range(2):
            lse1 = lse_rcv[s_z, a:a + 1]
            lse_n = lse2[s_z * 2 + a]
            high = jnp.maximum(lse1, lse_n)
            e1 = jnp.exp2(lse1 - high)
            e2 = jnp.exp2(lse_n - high)
            both = e1 + e2
            o1 = o_rcv[s_z, a, :, GROUP:].astype(jnp.float32)
            noisy = o1 * (e1 / both) + o2[s_z * 2 + a] * (e2 / both)
            side = slice(a * HEAD, (a + 1) * HEAD)
            ctx[s_z, :GROUP, side] = jnp.transpose(o_rcv[s_z, a, :, :GROUP], (1, 0))
            ctx[s_z, GROUP:, side] = jnp.transpose(noisy.astype(jnp.bfloat16), (1, 0))

    def project(steps, first, last):
        @pl.loop(0, w.shape[1] // TILE)
        def _(n):
            tile = pl.ds(pl.multiple_of(n * TILE, TILE), TILE)
            total = None if first else acc[:, tile]
            for t in steps:
                s_z = peer(t, -1)
                rows = w_all[pl.ds(s_z * 2, 2), :, tile].reshape(PAIR, TILE)
                term = jnp.dot(ctx[s_z], rows, preferred_element_type=jnp.float32)
                total = term if total is None else total + term
            if last:
                out[:, tile] = total.astype(jnp.bfloat16)
            else:
                acc[:, tile] = total

    for t in (0, 1, 2, 3):
        merge(t)
    local[6].wait()
    for i in range(HEADS // 2):
        for half in range(2):
            arrive(i * 2 + (fs + 1) % 2, half)
    project((0, 1, 2, 3), True, False)
    for t in (4, 5):
        merge(t)
    project((4, 5), False, False)
    for copy in started:
        copy.wait_send()

    @pl.loop(0, Z)
    def _(s):
        send_twin(s).wait_send()

    @pl.loop(1, Z)
    def _(t):
        j = peer(t, 1)
        send_k(j, z).wait_send()
        send_v(j, z).wait_send()
        send_q(j, z).wait_send()

    @pl.loop(1, 6)
    def _(t):
        j = peer(t, -1)
        send_o(j, z).wait_send()
        send_l(j, z).wait_send()

    for t in (6, 7):
        merge(t)
    project((6, 7), False, True)

    for t in (6, 7):
        send_o(peer(t, -1), z).wait_send()
        send_l(peer(t, -1), z).wait_send()


def local(queries, keys, values, docs, layout, w_out):
    def vm(*shape):
        return pltpu.VMEM(shape, jnp.bfloat16)

    def vf(*shape):
        return pltpu.VMEM(shape, jnp.float32)

    def dma(*shape):
        return pltpu.SemaphoreType.DMA(shape)

    width = w_out.shape[1]
    operands = [pltpu.with_memory_space_constraint(a, pltpu.HBM) for a in (layout, docs, queries, keys, values, w_out)]
    mixed = pl.pallas_call(
        kernel,
        out_shape=jax.ShapeDtypeStruct((2 * GROUP, width), jnp.bfloat16),
        in_specs=[pl.BlockSpec(memory_space=pltpu.HBM)] * 6,
        out_specs=pl.BlockSpec(memory_space=pltpu.VMEM),
        scratch_shapes=[
            pltpu.SMEM((N,), jnp.int32), pltpu.VMEM((1, N * GROUP), jnp.int32),
            vm(HEADS, HEAD, width), vm(Z, 2 * GROUP, PAIR), vf(2 * GROUP, width),
            vm(Z, 2, GROUP, PAIR), vm(N, 2, GROUP, PAIR), vm(N, PAIR, GROUP),
            vm(Z, 2, HEAD, 2 * GROUP), vf(Z, 2, GROUP), vm(Z, 2, HEAD, 2 * GROUP), vf(Z, 2, GROUP),
            vm(GROUP, HEADS * HEAD), vm(GROUP, HEADS * HEAD), vm(GROUP, HEADS * HEAD),
            vf(HEADS, HEAD, GROUP), vf(HEADS, 1, GROUP), vf(N, 1, GROUP), vf(N, GROUP, GROUP),
            vf(2, WINDOW, GROUP, 2 * GROUP), pltpu.SMEM((N,), jnp.int32),
            dma(Z, 2), dma(N, 2), dma(Z), dma(Z), dma(Z), dma(Z), dma(Z), dma(Z), dma(Z),
            dma(9), dma(30), dma(HEADS, 2),
        ],
        compiler_params=pltpu.CompilerParams(
            collective_id=0, has_side_effects=True, vmem_limit_bytes=48 * 2 ** 20),
        cost_estimate=pl.CostEstimate(flops=8 * 10 ** 9, bytes_accessed=8 * 10 ** 6, transcendentals=5 * 10 ** 6),
    )(*operands)
    return mixed.reshape(1, 2, GROUP, width)


def solution(mesh):
    return jax.shard_map(
        local,
        mesh=mesh,
        in_specs=(
            P("fsdp", None, "ctx", None),
            P("fsdp", None, "ctx", None),
            P("fsdp", None, "ctx", None),
            P("fsdp", None),
            P(),
            P("fsdp", None),
        ),
        out_specs=P("fsdp", None, "ctx", None),
        check_vma=False,
    )
```

```python
import math

import jax
import jax.numpy as jnp
from jax import lax
from jax.experimental import pallas as pl
from jax.experimental.pallas import tpu as pltpu
from jax.sharding import PartitionSpec as P

MESH = pl.DeviceIdType.MESH
HEAD = 128
GROUP = 128
BLOCK = 16
HEADS = 16
N = 16
Z = 8
PAIR = 2 * HEAD
WINDOW = 1024 // GROUP + 1
MASKED = -1e30
FLOOR = -1e20
TINY = 1e-30
C2 = math.log2(math.e) / math.sqrt(HEAD)
TILE = 2048
EARLY = 6


def shift(step):
    back = (Z - step) % Z
    return ((back + 1) // 2) * (1 - 2 * ((back + 1) % 2))


def peer(step, sign):
    return (lax.axis_index("ctx") // 2 + sign * shift(step) + Z) % Z


def slot_of(shard):
    d = (lax.axis_index("ctx") // 2 - shard // 2 + Z) % Z
    upper = d // (Z // 2 + 1)
    n = (1 - upper) * (2 * d - 1 + (Z - 1 - d) // (Z - 1)) + upper * 2 * (Z - d)
    return (Z - n) % Z * 2 + shard % 2


def column_of(row):
    return jnp.transpose(jnp.broadcast_to(row, (GROUP, row.shape[1])), (1, 0))


def kernel(
    layout_hbm, docs_hbm, q, k, v, w, acc, ctx_late, w_late,
    layout, docs, w_all, ctx, q_all, kv_all, vt_all, o_snd, lse_snd, o_rcv, lse_rcv,
    qn, kn, vn, o2, lse2, doc_rows, doc_cols, scores, inv,
    kv_ss, kv_rs, tw_ss, q_ss, q_rs, o_ss, o_rs, l_ss, l_rs, loc, w_ss, w_rs,
):
    me = lax.axis_index("ctx")
    fs = lax.axis_index("fsdp")
    z, yh = me // 2, me % 2
    twin = z * 2 + (yh + 1) % 2
    kin = (fs // 2) * 2 + (fs + 1) % 2
    across = (fs // 4) * 4 + (fs + 2) % 4
    right, left, far = (fs + 4) % N, (fs + 12) % N, (fs + 8) % N
    beside = {"kin": (me, kin), "right": (me, right), "left": (me, left), "near": (me, across), "away": (twin, across)}

    def pair(i):
        return pl.ds(pl.multiple_of(i * PAIR, PAIR), PAIR)

    def lanes(h):
        return pl.ds(pl.multiple_of(h * HEAD, HEAD), HEAD)

    def place(zz):
        return zz * 2 + yh

    barrier = pltpu.get_barrier_semaphore()
    for t in range(1, Z):
        pl.semaphore_signal(barrier, inc=1, device_id=(place(peer(t, 1)), fs), device_id_type=MESH)
    pl.semaphore_signal(barrier, inc=1, device_id=(twin, fs), device_id_type=MESH)
    for name in beside:
        pl.semaphore_signal(barrier, inc=1, device_id=beside[name], device_id_type=MESH)

    local = [
        pltpu.make_async_copy(k.at[0, 0, :, pair(z)], kv_all.at[me, 0], loc.at[0]),
        pltpu.make_async_copy(v.at[0, 0, :, pair(z)], kv_all.at[me, 1], loc.at[1]),
        pltpu.make_async_copy(q.at[0, :, :, pair(z)], q_all.at[z], loc.at[2]),
        pltpu.make_async_copy(q.at[0, 1], qn, loc.at[3]),
        pltpu.make_async_copy(k.at[0, 1], kn, loc.at[4]),
        pltpu.make_async_copy(v.at[0, 1], vn, loc.at[5]),
        pltpu.make_async_copy(w, w_all.at[slot_of(fs)], loc.at[6]),
        pltpu.make_async_copy(docs_hbm, docs, loc.at[7]),
        pltpu.make_async_copy(layout_hbm, layout, loc.at[8]),
    ]
    pl.semaphore_wait(barrier, Z + len(beside))

    def send_k(j, s):
        return pltpu.make_async_remote_copy(
            src_ref=k.at[0, 0, :, pair(j)], dst_ref=kv_all.at[place(s), 0], send_sem=kv_ss.at[j, 0],
            recv_sem=kv_rs.at[place(s), 0], device_id=(place(j), fs), device_id_type=MESH)

    def send_v(j, s):
        return pltpu.make_async_remote_copy(
            src_ref=v.at[0, 0, :, pair(j)], dst_ref=kv_all.at[place(s), 1], send_sem=kv_ss.at[j, 1],
            recv_sem=kv_rs.at[place(s), 1], device_id=(place(j), fs), device_id_type=MESH)

    def send_twin(s):
        return pltpu.make_async_remote_copy(
            src_ref=kv_all.at[place(s)], dst_ref=kv_all.at[place(s)], send_sem=tw_ss.at[s],
            recv_sem=kv_rs.at[place(s), 0], device_id=(twin, fs), device_id_type=MESH)

    def take_twin(s):
        slot = s * 2 + (yh + 1) % 2
        return pltpu.make_async_remote_copy(
            src_ref=kv_all.at[slot], dst_ref=kv_all.at[slot], send_sem=tw_ss.at[s],
            recv_sem=kv_rs.at[slot, 0], device_id=(twin, fs), device_id_type=MESH)

    def send_q(j, s):
        return pltpu.make_async_remote_copy(
            src_ref=q.at[0, :, :, pair(j)], dst_ref=q_all.at[s], send_sem=q_ss.at[j],
            recv_sem=q_rs.at[s], device_id=(place(j), fs), device_id_type=MESH)

    def send_o(j, s):
        return pltpu.make_async_remote_copy(
            src_ref=o_snd.at[j], dst_ref=o_rcv.at[s], send_sem=o_ss.at[j],
            recv_sem=o_rs.at[s], device_id=(place(j), fs), device_id_type=MESH)

    def send_l(j, s):
        return pltpu.make_async_remote_copy(
            src_ref=lse_snd.at[j], dst_ref=lse_rcv.at[s], send_sem=l_ss.at[j],
            recv_sem=l_rs.at[s], device_id=(place(j), fs), device_id_type=MESH)

    started = []

    def part(ref, half):
        return ref.at[pl.ds(half * GROUP // 2, GROUP // 2)]

    def pass_on(shard, half, name, own=False):
        copy = pltpu.make_async_remote_copy(
            src_ref=part(w if own else w_all.at[slot_of(shard)], half), dst_ref=part(w_all.at[slot_of(shard)], half),
            send_sem=w_ss.at[len(started)], recv_sem=w_rs.at[shard, half],
            device_id=beside[name], device_id_type=MESH)
        copy.start()
        started.append(copy)

    def arrive(shard, half):
        pltpu.make_async_remote_copy(
            src_ref=part(w_all.at[slot_of(shard)], half), dst_ref=part(w_all.at[slot_of(shard)], half),
            send_sem=w_ss.at[0], recv_sem=w_rs.at[shard, half],
            device_id=beside["kin"], device_id_type=MESH).wait_recv()

    @pl.loop(1, Z)
    def _(t):
        j = peer(t, 1)
        send_k(j, z).start()
        send_v(j, z).start()

    for i in (0, 1, 7, 8, 3, 4, 5, 2, 6):
        local[i].start()
    pass_on(fs, 0, "near", True)
    pass_on(fs, 1, "away", True)
    pass_on(fs, 0, "right", True)
    pass_on(fs, 1, "left", True)
    local[0].wait()
    local[1].wait()
    send_twin(z).start()
    pass_on(fs, 1, "right", True)
    pass_on(fs, 0, "left", True)

    @pl.loop(1, Z)
    def _(t):
        send_q(peer(t, 1), z).start()

    for half in range(2):
        pass_on(fs, half, "kin", True)

    local[7].wait()
    local[8].wait()
    for g in range(N):
        doc_rows[g] = docs[:, g * GROUP:(g + 1) * GROUP].astype(jnp.float32)

    @pl.loop(0, N)
    def _(g):
        found = jnp.int32(0)
        for c in range(N):
            found = jnp.where(layout[c] == g, c, found)
        inv[g] = found

    @pl.loop(0, N)
    def _(g):
        doc_cols[g] = column_of(doc_rows[g])

    key_block = lax.broadcasted_iota(jnp.int32, (GROUP, GROUP), 0) // BLOCK
    query_block = lax.broadcasted_iota(jnp.int32, (GROUP, GROUP), 1) // BLOCK

    for copy in local[3:6]:
        copy.wait()
    mine = layout[me]
    home = (doc_cols[mine] == doc_rows[mine]) & (key_block == query_block)

    @pl.loop(0, HEADS)
    def _(h):
        s = lax.dot_general(kn[:, lanes(h)], qn[:, lanes(h)], (((1,), (1,)), ((), ())),
                            preferred_element_type=jnp.float32)
        s = jnp.where(home, s, MASKED)
        top = jnp.max(s, axis=0, keepdims=True)
        p = jnp.exp2((s - top) * C2)
        total = jnp.sum(p, axis=0, keepdims=True)
        o = lax.dot_general(vn[:, lanes(h)], p.astype(jnp.bfloat16), (((0,), (0,)), ((), ())),
                            preferred_element_type=jnp.float32)
        o2[h] = o / total
        lse2[h] = top * C2 + jnp.log2(total)

    def relay(low, high):
        @pl.loop(low, high)
        def _(t):
            s = peer(t, -1)
            send_k(s, s).wait_recv()
            send_v(s, s).wait_recv()
            send_twin(s).start()

    relay(1, 3)
    arrive(left, 0)
    pass_on(left, 0, "right")
    arrive(right, 1)
    pass_on(right, 1, "left")
    relay(3, 5)
    arrive(across, 0)
    pass_on(across, 0, "right")
    arrive(across, 1)
    pass_on(across, 1, "left")
    pass_on(left, 0, "kin")
    pass_on(right, 1, "kin")
    relay(5, Z)
    arrive(left, 1)
    pass_on(left, 1, "away")
    arrive(right, 0)
    pass_on(right, 0, "near")
    pass_on(left, 1, "kin")
    pass_on(right, 0, "kin")
    for half in range(2):
        pass_on(across, half, "kin")

    def turn(g):
        vt_all[g] = jnp.transpose(kv_all[g, 1].astype(jnp.float32), (1, 0)).astype(jnp.bfloat16)

    @pl.loop(0, Z)
    def _(zz):
        turn(place(zz))

    @pl.loop(0, Z)
    def _(t):
        s = peer(t, -1)
        take_twin(s).wait_recv()
        turn(s * 2 + (yh + 1) % 2)

    local[2].wait()

    def attend(t):
        s_z = peer(t, -1)

        @pl.when(t > 0)
        def _():
            send_q(s_z, s_z).wait_recv()

        p_q = layout[place(s_z)]
        doc_q = doc_rows[p_q]
        tops = [jnp.full((1, 2 * GROUP), FLOOR, jnp.float32)] * 2
        queries = [q_all[s_z, :, :, a * HEAD:(a + 1) * HEAD].reshape(2 * GROUP, HEAD) for a in range(2)]
        places = []
        for w_ in range(WINDOW):
            at = (p_q - w_ + N) % N
            where = inv[at]
            places.append(where)
            wanted = jnp.where(p_q >= w_, doc_q, -1.0)
            same = doc_cols[at] == wanted
            if w_ == 0:
                clean = same & (key_block <= query_block)
                noisy = same & (key_block < query_block)
            else:
                clean = noisy = same
            for a in range(2):
                s = lax.dot_general(kv_all[where, 0, :, a * HEAD:(a + 1) * HEAD], queries[a],
                                    (((1,), (1,)), ((), ())), preferred_element_type=jnp.float32)
                s = jnp.concatenate(
                    [jnp.where(clean, s[:, :GROUP], MASKED), jnp.where(noisy, s[:, GROUP:], MASKED)], axis=1)
                scores[a, w_] = s
                tops[a] = jnp.maximum(tops[a], jnp.max(s, axis=0, keepdims=True))
        for a in range(2):
            top = tops[a]
            total = jnp.zeros((1, 2 * GROUP), jnp.float32)
            o = jnp.zeros((HEAD, 2 * GROUP), jnp.float32)
            for w_ in range(WINDOW):
                p = jnp.exp2((scores[a, w_] - top) * C2)
                total = total + jnp.sum(p, axis=0, keepdims=True)
                o = o + jnp.dot(vt_all[places[w_], a * HEAD:(a + 1) * HEAD], p.astype(jnp.bfloat16),
                                preferred_element_type=jnp.float32)
            safe = jnp.maximum(total, TINY)
            o_snd[s_z, a] = (o / safe).astype(jnp.bfloat16)
            lse = top * C2 + jnp.log2(safe)
            lse_snd[s_z, a:a + 1] = lse[:, GROUP:]

        @pl.when(t > 0)
        def _():
            send_o(s_z, z).start()
            send_l(s_z, z).start()

        @pl.when(t == 0)
        def _():
            o_rcv[z] = o_snd[s_z]
            lse_rcv[z] = lse_snd[s_z]

    @pl.loop(0, Z // 2)
    def _(t):
        attend(t)

    arrive(far, 0)
    pass_on(far, 0, "near")
    arrive(far, 1)
    pass_on(far, 1, "away")
    for half in range(2):
        pass_on(far, half, "kin")

    @pl.loop(Z // 2, Z)
    def _(t):
        attend(t)

    for shard in ((across + 4) % N, (across + 12) % N, (across + 8) % N):
        for half in range(2):
            arrive(shard, half)
            pass_on(shard, half, "kin")

    def merge(t):
        s_z = peer(t, -1)
        if t > 0:
            send_o(s_z, s_z).wait_recv()
            send_l(s_z, s_z).wait_recv()
        for a in range(2):
            lse1 = lse_rcv[s_z, a:a + 1]
            lse_n = lse2[s_z * 2 + a]
            high = jnp.maximum(lse1, lse_n)
            e1 = jnp.exp2(lse1 - high)
            e2 = jnp.exp2(lse_n - high)
            both = e1 + e2
            o1 = o_rcv[s_z, a, :, GROUP:].astype(jnp.float32)
            noisy = o1 * (e1 / both) + o2[s_z * 2 + a] * (e2 / both)
            side = slice((t * 2 + a) * HEAD, (t * 2 + a + 1) * HEAD)
            held = ctx
            if t >= EARLY:
                held = ctx_late
                side = slice(((t - EARLY) * 2 + a) * HEAD, ((t - EARLY) * 2 + a + 1) * HEAD)
            held[:GROUP, side] = jnp.transpose(o_rcv[s_z, a, :, :GROUP], (1, 0))
            held[GROUP:, side] = jnp.transpose(noisy.astype(jnp.bfloat16), (1, 0))

    def project(steps, first):
        low, high = steps[0], steps[-1] + 1

        @pl.loop(0, w.shape[1] // TILE)
        def _(n):
            tile = pl.ds(pl.multiple_of(n * TILE, TILE), TILE)
            rows = w_all[2 * low:2 * high, :, tile].reshape((high - low) * PAIR, TILE)
            total = jnp.dot(ctx[:, low * PAIR:high * PAIR], rows, preferred_element_type=jnp.float32)
            if not first:
                total = total + acc[:, tile]
            acc[:, tile] = total

    for t in (0, 1, 2, 3):
        merge(t)
    local[6].wait()
    for i in range(HEADS // 2):
        for half in range(2):
            arrive(i * 2 + (fs + 1) % 2, half)
    late = pltpu.make_async_copy(w_all.at[pl.ds(2 * EARLY, HEADS - 2 * EARLY)], w_late, loc.at[9])
    late.start()
    project((0, 1, 2, 3), True)
    for t in (4, 5):
        merge(t)
    project((4, 5), False)
    late.wait()
    for copy in started:
        copy.wait_send()

    @pl.loop(0, Z)
    def _(s):
        send_twin(s).wait_send()

    @pl.loop(1, Z)
    def _(t):
        j = peer(t, 1)
        send_k(j, z).wait_send()
        send_v(j, z).wait_send()
        send_q(j, z).wait_send()

    @pl.loop(1, 6)
    def _(t):
        j = peer(t, -1)
        send_o(j, z).wait_send()
        send_l(j, z).wait_send()

    for t in (6, 7):
        merge(t)

    for t in (6, 7):
        send_o(peer(t, -1), z).wait_send()
        send_l(peer(t, -1), z).wait_send()


def local(queries, keys, values, docs, layout, w_out):
    def vm(*shape):
        return pltpu.VMEM(shape, jnp.bfloat16)

    def vf(*shape):
        return pltpu.VMEM(shape, jnp.float32)

    def dma(*shape):
        return pltpu.SemaphoreType.DMA(shape)

    width = w_out.shape[1]
    operands = [pltpu.with_memory_space_constraint(a, pltpu.HBM) for a in (layout, docs, queries, keys, values, w_out)]
    acc, ctx_late, w_late = pl.pallas_call(
        kernel,
        out_shape=(
            jax.ShapeDtypeStruct((2 * GROUP, width), jnp.float32),
            jax.ShapeDtypeStruct((2 * GROUP, (Z - EARLY) * PAIR), jnp.bfloat16),
            jax.ShapeDtypeStruct((HEADS - 2 * EARLY, HEAD, width), jnp.bfloat16),
        ),
        in_specs=[pl.BlockSpec(memory_space=pltpu.HBM)] * 6,
        out_specs=[pl.BlockSpec(memory_space=pltpu.VMEM)] * 3,
        scratch_shapes=[
            pltpu.SMEM((N,), jnp.int32), pltpu.VMEM((1, N * GROUP), jnp.int32),
            vm(HEADS, HEAD, width), vm(2 * GROUP, EARLY * PAIR),
            vm(Z, 2, GROUP, PAIR), vm(N, 2, GROUP, PAIR), vm(N, PAIR, GROUP),
            vm(Z, 2, HEAD, 2 * GROUP), vf(Z, 2, GROUP), vm(Z, 2, HEAD, 2 * GROUP), vf(Z, 2, GROUP),
            vm(GROUP, HEADS * HEAD), vm(GROUP, HEADS * HEAD), vm(GROUP, HEADS * HEAD),
            vf(HEADS, HEAD, GROUP), vf(HEADS, 1, GROUP), vf(N, 1, GROUP), vf(N, GROUP, GROUP),
            vf(2, WINDOW, GROUP, 2 * GROUP), pltpu.SMEM((N,), jnp.int32),
            dma(Z, 2), dma(N, 2), dma(Z), dma(Z), dma(Z), dma(Z), dma(Z), dma(Z), dma(Z),
            dma(10), dma(30), dma(HEADS, 2),
        ],
        compiler_params=pltpu.CompilerParams(
            collective_id=0, has_side_effects=True, vmem_limit_bytes=40 * 2 ** 20),
        cost_estimate=pl.CostEstimate(flops=8 * 10 ** 9, bytes_accessed=8 * 10 ** 6, transcendentals=5 * 10 ** 6),
    )(*operands)
    rows = w_late.reshape((Z - EARLY) * PAIR, width)
    mixed = acc + jnp.dot(ctx_late, rows, preferred_element_type=jnp.float32)
    return mixed.astype(jnp.bfloat16).reshape(1, 2, GROUP, width)


def solution(mesh):
    return jax.shard_map(
        local,
        mesh=mesh,
        in_specs=(
            P("fsdp", None, "ctx", None),
            P("fsdp", None, "ctx", None),
            P("fsdp", None, "ctx", None),
            P("fsdp", None),
            P(),
            P("fsdp", None),
        ),
        out_specs=P("fsdp", None, "ctx", None),
        check_vma=False,
    )
```

```python
import math

import jax
import jax.numpy as jnp
from jax import lax
from jax.experimental import pallas as pl
from jax.experimental.pallas import tpu as pltpu
from jax.sharding import PartitionSpec as P

MESH = pl.DeviceIdType.MESH
HEAD = 128
GROUP = 128
BLOCK = 16
HEADS = 16
N = 16
Z = 8
PAIR = 2 * HEAD
WINDOW = 1024 // GROUP + 1
MASKED = -1e30
FLOOR = -1e20
TINY = 1e-30
C2 = math.log2(math.e) / math.sqrt(HEAD)
TILE = 2048


def shift(step):
    back = (Z - step) % Z
    return ((back + 1) // 2) * (1 - 2 * ((back + 1) % 2))


def peer(step, sign):
    return (lax.axis_index("ctx") // 2 + sign * shift(step) + Z) % Z


def column_of(row):
    return jnp.transpose(jnp.broadcast_to(row, (GROUP, row.shape[1])), (1, 0))


def kernel(
    layout_hbm, docs_hbm, q, k, v, w, out,
    layout, docs, kv_src, q_src, w_all, ctx, acc, q_all, kv_all, vt_all, o_snd, lse_snd, o_rcv, lse_rcv,
    qn, kn, vn, o2, lse2, doc_rows, doc_cols, scores, inv,
    kv_ss, kv_rs, tw_ss, q_ss, q_rs, o_ss, o_rs, l_ss, l_rs, loc, w_ss, w_rs, stage,
):
    me = lax.axis_index("ctx")
    fs = lax.axis_index("fsdp")
    z, yh = me // 2, me % 2
    twin = z * 2 + (yh + 1) % 2
    kin = (fs // 2) * 2 + (fs + 1) % 2
    across = (fs // 4) * 4 + (fs + 2) % 4
    right, left, far = (fs + 4) % N, (fs + 12) % N, (fs + 8) % N
    beside = {"kin": (me, kin), "right": (me, right), "left": (me, left), "near": (me, across), "away": (twin, across)}

    def pair(i):
        return pl.ds(pl.multiple_of(i * PAIR, PAIR), PAIR)

    def lanes(h):
        return pl.ds(pl.multiple_of(h * HEAD, HEAD), HEAD)

    def place(zz):
        return zz * 2 + yh

    barrier = pltpu.get_barrier_semaphore()
    for t in range(1, Z):
        pl.semaphore_signal(barrier, inc=1, device_id=(place(peer(t, 1)), fs), device_id_type=MESH)
    pl.semaphore_signal(barrier, inc=1, device_id=(twin, fs), device_id_type=MESH)
    for name in beside:
        pl.semaphore_signal(barrier, inc=1, device_id=beside[name], device_id_type=MESH)

    local = [
        pltpu.make_async_copy(k.at[0, 0, :, pair(z)], kv_all.at[me, 0], loc.at[0]),
        pltpu.make_async_copy(v.at[0, 0, :, pair(z)], kv_all.at[me, 1], loc.at[1]),
        pltpu.make_async_copy(q.at[0, :, :, pair(z)], q_all.at[z], loc.at[2]),
        pltpu.make_async_copy(q.at[0, 1], qn, loc.at[3]),
        pltpu.make_async_copy(k.at[0, 1], kn, loc.at[4]),
        pltpu.make_async_copy(v.at[0, 1], vn, loc.at[5]),
        pltpu.make_async_copy(w, w_all.at[fs], loc.at[6]),
        pltpu.make_async_copy(docs_hbm, docs, loc.at[7]),
        pltpu.make_async_copy(layout_hbm, layout, loc.at[8]),
    ]
    def staged(j):
        return [
            pltpu.make_async_copy(k.at[0, 0, :, pair(j)], kv_src.at[j, 0], stage.at[j, 0]),
            pltpu.make_async_copy(v.at[0, 0, :, pair(j)], kv_src.at[j, 1], stage.at[j, 1]),
            pltpu.make_async_copy(q.at[0, :, :, pair(j)], q_src.at[j], stage.at[j, 2]),
        ]

    @pl.loop(1, Z)
    def _(t):
        for copy in staged(peer(t, 1)):
            copy.start()

    pl.semaphore_wait(barrier, Z + len(beside))

    def send_kv(j, s):
        return pltpu.make_async_remote_copy(
            src_ref=kv_src.at[j], dst_ref=kv_all.at[place(s)], send_sem=kv_ss.at[j, 0],
            recv_sem=kv_rs.at[place(s), 0], device_id=(place(j), fs), device_id_type=MESH)

    def send_twin(s):
        return pltpu.make_async_remote_copy(
            src_ref=kv_all.at[place(s)], dst_ref=kv_all.at[place(s)], send_sem=tw_ss.at[s],
            recv_sem=kv_rs.at[place(s), 0], device_id=(twin, fs), device_id_type=MESH)

    def take_twin(s):
        slot = s * 2 + (yh + 1) % 2
        return pltpu.make_async_remote_copy(
            src_ref=kv_all.at[slot], dst_ref=kv_all.at[slot], send_sem=tw_ss.at[s],
            recv_sem=kv_rs.at[slot, 0], device_id=(twin, fs), device_id_type=MESH)

    def send_q(j, s):
        return pltpu.make_async_remote_copy(
            src_ref=q_src.at[j], dst_ref=q_all.at[s], send_sem=q_ss.at[j],
            recv_sem=q_rs.at[s], device_id=(place(j), fs), device_id_type=MESH)

    def send_o(j, s):
        return pltpu.make_async_remote_copy(
            src_ref=o_snd.at[j], dst_ref=o_rcv.at[s], send_sem=o_ss.at[j],
            recv_sem=o_rs.at[s], device_id=(place(j), fs), device_id_type=MESH)

    def send_l(j, s):
        return pltpu.make_async_remote_copy(
            src_ref=lse_snd.at[j], dst_ref=lse_rcv.at[s], send_sem=l_ss.at[j],
            recv_sem=l_rs.at[s], device_id=(place(j), fs), device_id_type=MESH)

    started = []

    def part(ref, half):
        return ref.at[pl.ds(half * GROUP // 2, GROUP // 2)]

    def pass_on(shard, half, name, own=False):
        copy = pltpu.make_async_remote_copy(
            src_ref=part(w if own else w_all.at[shard], half), dst_ref=part(w_all.at[shard], half),
            send_sem=w_ss.at[len(started)], recv_sem=w_rs.at[shard, half],
            device_id=beside[name], device_id_type=MESH)
        copy.start()
        started.append(copy)

    def arrive(shard, half):
        pltpu.make_async_remote_copy(
            src_ref=part(w_all.at[shard], half), dst_ref=part(w_all.at[shard], half),
            send_sem=w_ss.at[0], recv_sem=w_rs.at[shard, half],
            device_id=beside["kin"], device_id_type=MESH).wait_recv()

    @pl.loop(1, Z)
    def _(t):
        j = peer(t, 1)
        for copy in staged(j)[:2]:
            copy.wait()
        send_kv(j, z).start()

    for i in (0, 1, 7, 8, 3, 4, 5, 2, 6):
        local[i].start()
    pass_on(fs, 0, "near", True)
    pass_on(fs, 1, "away", True)
    pass_on(fs, 0, "right", True)
    pass_on(fs, 1, "left", True)
    local[0].wait()
    local[1].wait()
    send_twin(z).start()
    pass_on(fs, 1, "right", True)
    pass_on(fs, 0, "left", True)

    @pl.loop(1, Z)
    def _(t):
        staged(peer(t, 1))[2].wait()
        send_q(peer(t, 1), z).start()

    for half in range(2):
        pass_on(fs, half, "kin", True)

    local[7].wait()
    local[8].wait()
    for g in range(N):
        doc_rows[g] = docs[:, g * GROUP:(g + 1) * GROUP].astype(jnp.float32)

    @pl.loop(0, N)
    def _(g):
        found = jnp.int32(0)
        for c in range(N):
            found = jnp.where(layout[c] == g, c, found)
        inv[g] = found

    @pl.loop(0, N)
    def _(g):
        doc_cols[g] = column_of(doc_rows[g])

    key_block = lax.broadcasted_iota(jnp.int32, (GROUP, GROUP), 0) // BLOCK
    query_block = lax.broadcasted_iota(jnp.int32, (GROUP, GROUP), 1) // BLOCK

    for copy in local[3:6]:
        copy.wait()
    mine = layout[me]
    home = (doc_cols[mine] == doc_rows[mine]) & (key_block == query_block)

    @pl.loop(0, HEADS)
    def _(h):
        s = lax.dot_general(kn[:, lanes(h)], qn[:, lanes(h)], (((1,), (1,)), ((), ())),
                            preferred_element_type=jnp.float32)
        s = jnp.where(home, s, MASKED)
        top = jnp.max(s, axis=0, keepdims=True)
        p = jnp.exp2((s - top) * C2)
        total = jnp.sum(p, axis=0, keepdims=True)
        o = lax.dot_general(vn[:, lanes(h)], p.astype(jnp.bfloat16), (((0,), (0,)), ((), ())),
                            preferred_element_type=jnp.float32)
        o2[h] = o / total
        lse2[h] = top * C2 + jnp.log2(total)

    def relay(low, high):
        @pl.loop(low, high)
        def _(t):
            s = peer(t, -1)
            send_kv(s, s).wait_recv()
            send_twin(s).start()

    relay(1, 3)
    arrive(left, 0)
    pass_on(left, 0, "right")
    arrive(right, 1)
    pass_on(right, 1, "left")
    relay(3, 5)
    arrive(across, 0)
    pass_on(across, 0, "right")
    arrive(across, 1)
    pass_on(across, 1, "left")
    pass_on(left, 0, "kin")
    pass_on(right, 1, "kin")
    relay(5, Z)
    arrive(left, 1)
    pass_on(left, 1, "away")
    arrive(right, 0)
    pass_on(right, 0, "near")
    pass_on(left, 1, "kin")
    pass_on(right, 0, "kin")
    for half in range(2):
        pass_on(across, half, "kin")

    def turn(g):
        vt_all[g] = jnp.transpose(kv_all[g, 1].astype(jnp.float32), (1, 0)).astype(jnp.bfloat16)

    @pl.loop(0, Z)
    def _(zz):
        turn(place(zz))

    @pl.loop(0, Z)
    def _(t):
        s = peer(t, -1)
        take_twin(s).wait_recv()
        turn(s * 2 + (yh + 1) % 2)

    local[2].wait()

    def attend(t):
        s_z = peer(t, -1)

        @pl.when(t > 0)
        def _():
            send_q(s_z, s_z).wait_recv()

        p_q = layout[place(s_z)]
        doc_q = doc_rows[p_q]
        tops = [jnp.full((1, 2 * GROUP), FLOOR, jnp.float32)] * 2
        queries = [q_all[s_z, :, :, a * HEAD:(a + 1) * HEAD].reshape(2 * GROUP, HEAD) for a in range(2)]
        places = []
        for w_ in range(WINDOW):
            at = (p_q - w_ + N) % N
            where = inv[at]
            places.append(where)
            wanted = jnp.where(p_q >= w_, doc_q, -1.0)
            same = doc_cols[at] == wanted
            if w_ == 0:
                clean = same & (key_block <= query_block)
                noisy = same & (key_block < query_block)
            else:
                clean = noisy = same
            for a in range(2):
                s = lax.dot_general(kv_all[where, 0, :, a * HEAD:(a + 1) * HEAD], queries[a],
                                    (((1,), (1,)), ((), ())), preferred_element_type=jnp.float32)
                s = jnp.concatenate(
                    [jnp.where(clean, s[:, :GROUP], MASKED), jnp.where(noisy, s[:, GROUP:], MASKED)], axis=1)
                scores[a, w_] = s
                tops[a] = jnp.maximum(tops[a], jnp.max(s, axis=0, keepdims=True))
        for a in range(2):
            top = tops[a]
            total = jnp.zeros((1, 2 * GROUP), jnp.float32)
            o = jnp.zeros((HEAD, 2 * GROUP), jnp.float32)
            for w_ in range(WINDOW):
                p = jnp.exp2((scores[a, w_] - top) * C2)
                total = total + jnp.sum(p, axis=0, keepdims=True)
                o = o + jnp.dot(vt_all[places[w_], a * HEAD:(a + 1) * HEAD], p.astype(jnp.bfloat16),
                                preferred_element_type=jnp.float32)
            safe = jnp.maximum(total, TINY)
            o_snd[s_z, a] = (o / safe).astype(jnp.bfloat16)
            lse = top * C2 + jnp.log2(safe)
            lse_snd[s_z, a:a + 1] = lse[:, GROUP:]

        @pl.when(t > 0)
        def _():
            send_o(s_z, z).start()
            send_l(s_z, z).start()

        @pl.when(t == 0)
        def _():
            o_rcv[z] = o_snd[s_z]
            lse_rcv[z] = lse_snd[s_z]

    @pl.loop(0, Z // 2)
    def _(t):
        attend(t)

    arrive(far, 0)
    pass_on(far, 0, "near")
    arrive(far, 1)
    pass_on(far, 1, "away")
    for half in range(2):
        pass_on(far, half, "kin")

    @pl.loop(Z // 2, Z)
    def _(t):
        attend(t)

    for shard in ((across + 4) % N, (across + 12) % N, (across + 8) % N):
        for half in range(2):
            arrive(shard, half)
            pass_on(shard, half, "kin")

    def merge(t):
        s_z = peer(t, -1)
        if t > 0:
            send_o(s_z, s_z).wait_recv()
            send_l(s_z, s_z).wait_recv()
        for a in range(2):
            lse1 = lse_rcv[s_z, a:a + 1]
            lse_n = lse2[s_z * 2 + a]
            high = jnp.maximum(lse1, lse_n)
            e1 = jnp.exp2(lse1 - high)
            e2 = jnp.exp2(lse_n - high)
            both = e1 + e2
            o1 = o_rcv[s_z, a, :, GROUP:].astype(jnp.float32)
            noisy = o1 * (e1 / both) + o2[s_z * 2 + a] * (e2 / both)
            side = slice(a * HEAD, (a + 1) * HEAD)
            ctx[s_z, :GROUP, side] = jnp.transpose(o_rcv[s_z, a, :, :GROUP], (1, 0))
            ctx[s_z, GROUP:, side] = jnp.transpose(noisy.astype(jnp.bfloat16), (1, 0))

    def project(steps, first, last):
        @pl.loop(0, w.shape[1] // TILE)
        def _(n):
            tile = pl.ds(pl.multiple_of(n * TILE, TILE), TILE)
            total = None if first else acc[:, tile]
            for t in steps:
                s_z = peer(t, -1)
                rows = w_all[pl.ds(s_z * 2, 2), :, tile].reshape(PAIR, TILE)
                term = jnp.dot(ctx[s_z], rows, preferred_element_type=jnp.float32)
                total = term if total is None else total + term
            if last:
                out[:, tile] = total.astype(jnp.bfloat16)
            else:
                acc[:, tile] = total

    for t in (0, 1, 2, 3):
        merge(t)
    local[6].wait()
    for i in range(HEADS // 2):
        for half in range(2):
            arrive(i * 2 + (fs + 1) % 2, half)
    project((0, 1, 2, 3), True, False)
    for t in (4, 5):
        merge(t)
    project((4, 5), False, False)
    for copy in started:
        copy.wait_send()

    @pl.loop(0, Z)
    def _(s):
        send_twin(s).wait_send()

    @pl.loop(1, Z)
    def _(t):
        j = peer(t, 1)
        send_kv(j, z).wait_send()
        send_q(j, z).wait_send()

    @pl.loop(1, 6)
    def _(t):
        j = peer(t, -1)
        send_o(j, z).wait_send()
        send_l(j, z).wait_send()

    for t in (6, 7):
        merge(t)
    project((6, 7), False, True)

    for t in (6, 7):
        send_o(peer(t, -1), z).wait_send()
        send_l(peer(t, -1), z).wait_send()


def local(queries, keys, values, docs, layout, w_out):
    def vm(*shape):
        return pltpu.VMEM(shape, jnp.bfloat16)

    def vf(*shape):
        return pltpu.VMEM(shape, jnp.float32)

    def dma(*shape):
        return pltpu.SemaphoreType.DMA(shape)

    width = w_out.shape[1]
    operands = [pltpu.with_memory_space_constraint(a, pltpu.HBM) for a in (layout, docs, queries, keys, values, w_out)]
    mixed = pl.pallas_call(
        kernel,
        out_shape=jax.ShapeDtypeStruct((2 * GROUP, width), jnp.bfloat16),
        in_specs=[pl.BlockSpec(memory_space=pltpu.HBM)] * 6,
        out_specs=pl.BlockSpec(memory_space=pltpu.VMEM),
        scratch_shapes=[
            pltpu.SMEM((N,), jnp.int32), pltpu.VMEM((1, N * GROUP), jnp.int32),
            vm(Z, 2, GROUP, PAIR), vm(Z, 2, GROUP, PAIR),
            vm(HEADS, HEAD, width), vm(Z, 2 * GROUP, PAIR), vf(2 * GROUP, width),
            vm(Z, 2, GROUP, PAIR), vm(N, 2, GROUP, PAIR), vm(N, PAIR, GROUP),
            vm(Z, 2, HEAD, 2 * GROUP), vf(Z, 2, GROUP), vm(Z, 2, HEAD, 2 * GROUP), vf(Z, 2, GROUP),
            vm(GROUP, HEADS * HEAD), vm(GROUP, HEADS * HEAD), vm(GROUP, HEADS * HEAD),
            vf(HEADS, HEAD, GROUP), vf(HEADS, 1, GROUP), vf(N, 1, GROUP), vf(N, GROUP, GROUP),
            vf(2, WINDOW, GROUP, 2 * GROUP), pltpu.SMEM((N,), jnp.int32),
            dma(Z, 2), dma(N, 2), dma(Z), dma(Z), dma(Z), dma(Z), dma(Z), dma(Z), dma(Z),
            dma(9), dma(30), dma(HEADS, 2), dma(Z, 3),
        ],
        compiler_params=pltpu.CompilerParams(
            collective_id=0, has_side_effects=True, vmem_limit_bytes=48 * 2 ** 20),
        cost_estimate=pl.CostEstimate(flops=8 * 10 ** 9, bytes_accessed=8 * 10 ** 6, transcendentals=5 * 10 ** 6),
    )(*operands)
    return mixed.reshape(1, 2, GROUP, width)


def solution(mesh):
    return jax.shard_map(
        local,
        mesh=mesh,
        in_specs=(
            P("fsdp", None, "ctx", None),
            P("fsdp", None, "ctx", None),
            P("fsdp", None, "ctx", None),
            P("fsdp", None),
            P(),
            P("fsdp", None),
        ),
        out_specs=P("fsdp", None, "ctx", None),
        check_vma=False,
    )
```
